256 devices in a mesh: ctx: 128 (over x, y_lo, z, core), head: 2 (over y_hi).
Axes of the slice: x: 4, y: 4 (y_hi: 2, y_lo: 2; y = y_hi * 2 + y_lo), z: 8, core: 2. Of those that a mesh axis runs over, the one named last changes fastest.
Arguments:
- queries: bfloat16 [16384, 2048], P('ctx', 'head'), may hold values from -5 to 5
- key_vectors: bfloat16 [16384, 2048], P('ctx', 'head'), may hold values from -5 to 5
- value_vectors: bfloat16 [16384, 2048], P('ctx', 'head'), may hold values from -12 to 12
- slopes: float32 [16], P('head'), may hold values from 0.15 to 1.5
- w_out: bfloat16 [2048, 2048], P('head'), may hold values from -0.125 to 0.125
- grad_out: bfloat16 [16384, 2048], P('ctx', 'head'), may hold values from -6 to 6
Outputs:
- layer_out: bfloat16 [16384, 2048], P('ctx', 'head')
- grad_queries: bfloat16 [16384, 2048], P('ctx', 'head')
- grad_keys: bfloat16 [16384, 2048], P('ctx', 'head')
- grad_values: bfloat16 [16384, 2048], P('ctx', 'head')
The draws below stay inside these ranges and needn't reach their ends.
All inputs are finite; a program needn't handle non-finite values.
Results may differ from the reference program's by a relative error of at most 0.008.
Values may be sent and summed in bfloat16 or wider, within the bound.
A program may use at most 128 MiB of HBM per device.

```python
import math
import jax
import jax.numpy as jnp
from jax import lax

HEADS = 16
HEAD_DIM = 128
D = 2048
B = 128
TOKENS = 16384
LEVELS = 7


def draw_queries(key, part):
    key = jax.random.fold_in(key, 11)
    drawn = jnp.clip(jax.random.normal(key, (TOKENS, D), jnp.float32), -5.0, 5.0)
    return drawn.astype(jnp.bfloat16)


def draw_key_vectors(key, part):
    key = jax.random.fold_in(key, 23)
    span = 2 ** (LEVELS - 1)
    key_span, key_rest = jax.random.split(key)
    span_part = jax.random.normal(key_span, (TOKENS // span, D), jnp.float32)
    rest_part = jax.random.normal(key_rest, (TOKENS, D), jnp.float32)
    drawn = jnp.clip(0.9 * jnp.repeat(span_part, span, axis=0) + 0.7 * rest_part, -5.0, 5.0)
    return drawn.astype(jnp.bfloat16)


def draw_value_vectors(key, part):
    key = jax.random.fold_in(key, 37)
    span = 2 ** (LEVELS - 1)
    key_span, key_rest = jax.random.split(key)
    span_part = jax.random.normal(key_span, (TOKENS // span, D), jnp.float32)
    rest_part = jax.random.normal(key_rest, (TOKENS, D), jnp.float32)
    drawn = jnp.clip(1.6 * jnp.repeat(span_part, span, axis=0) + 1.2 * rest_part, -12.0, 12.0)
    return drawn.astype(jnp.bfloat16)


def block_scale(key, shape, cuts, smallest, high):
    loudness = 1.0
    for axis_at, parts in cuts:
        heights = jax.random.uniform(jax.random.fold_in(jax.random.fold_in(key, 6), axis_at), (parts,), jnp.float32, smallest / len(cuts), high / len(cuts))
        loudness = loudness * jnp.repeat(jnp.exp(heights), shape[axis_at] // parts).reshape((-1,) + (1,) * (len(shape) - 1 - axis_at))
    return loudness


def centred(own_key, dims, spread, reach, shards=(), held_as=jnp.bfloat16):
    result = jax.random.normal(own_key, dims, jnp.float32) * spread
    if len(shards) > 0:
        result = block_scale(own_key, dims, shards, -0.22, 0.18) * result
    return jnp.clip(result, min=-reach, max=reach).astype(held_as)


def setup_inputs(seed: int = 0) -> dict:
    keys = jax.random.split(jax.random.key(seed), 7)
    return {
        "queries": draw_queries(jax.random.fold_in(keys[6], 71), 0),
        "key_vectors": draw_key_vectors(jax.random.fold_in(keys[6], 71), 0),
        "value_vectors": draw_value_vectors(jax.random.fold_in(keys[6], 71), 0),
        "slopes": jnp.clip(jnp.exp(math.log(1.5) - 2.3025851 * jax.random.uniform(keys[3], (HEADS,), jnp.float32) ** block_scale(keys[3], (HEADS,), ((0, 2),), -0.2, 0.2)), 0.15, 1.5),
        "w_out": centred(keys[4], (D, D), D ** -0.5, 0.125, ((0, 2),)),
        "grad_out": centred(keys[5], (TOKENS, D), 1.0, 6.0, ((0, 128), (1, 2))),
    }


LOG_TWO = math.log(2.0)

def pool_pairs(summary):
    paired = summary.astype(jnp.float32).reshape((summary.shape[0] // 2, 2) + summary.shape[1:])
    return lax.optimization_barrier((0.5 * (paired[:, 0] + paired[:, 1])).astype(jnp.bfloat16))

def unpool_pairs(gradient):
    return 0.5 * jnp.repeat(gradient, 2, axis=0)

def swap_pairs(grouped):
    paired = grouped.reshape((grouped.shape[0] // 2, 2) + grouped.shape[1:])
    return paired[:, ::-1].reshape(grouped.shape)

def attend(queries, groups_k, groups_v, biases, grad_attn):
    row_count, head_count, head_width = queries.shape
    inv_root = 1.0 / math.sqrt(head_width)
    query_f = queries.astype(jnp.float32)
    grad_f = grad_attn.astype(jnp.float32)
    score_list = []
    for keys_now, bias_now in zip(groups_k, biases):
        group_count = keys_now.shape[0]
        query_groups = query_f.reshape(group_count, row_count // group_count, head_count, head_width)
        scores_now = jnp.einsum('gqhd,gkhd->hgqk', query_groups, keys_now.astype(jnp.float32))
        score_list.append(scores_now.reshape(head_count, row_count, keys_now.shape[1]) * inv_root + bias_now[:, None, None])
    stacked = jnp.stack(score_list)
    row_max = lax.optimization_barrier(jnp.max(stacked, axis=(0, 3), keepdims=True))
    exp_scores = jnp.exp(stacked - row_max)
    weights = exp_scores / lax.optimization_barrier(jnp.sum(exp_scores, axis=(0, 3), keepdims=True))
    rounded = lax.optimization_barrier(weights.astype(jnp.bfloat16)).astype(jnp.float32)
    attn_sum = jnp.zeros((row_count, head_count, head_width), jnp.float32)
    grad_list = []
    for level_index, values_now in enumerate(groups_v):
        group_count = values_now.shape[0]
        per_group = row_count // group_count
        values_f = values_now.astype(jnp.float32)
        weight_now = rounded[level_index].reshape(head_count, group_count, per_group, values_now.shape[1])
        attn_sum = attn_sum + jnp.einsum('hgqk,gkhd->gqhd', weight_now, values_f).reshape(row_count, head_count, head_width)
        grad_groups = grad_f.reshape(group_count, per_group, head_count, head_width)
        grad_list.append(jnp.einsum('gqhd,gkhd->hgqk', grad_groups, values_f).reshape(head_count, row_count, values_now.shape[1]))
    grad_weights = jnp.stack(grad_list)
    center = lax.optimization_barrier(jnp.sum(weights * grad_weights, axis=(0, 3), keepdims=True))
    grad_scores = weights * (grad_weights - center)
    rounded_grad = lax.optimization_barrier(grad_scores.astype(jnp.bfloat16)).astype(jnp.float32)
    query_sum = jnp.zeros((row_count, head_count, head_width), jnp.float32)
    key_grads = []
    value_grads = []
    for level_index, keys_now in enumerate(groups_k):
        group_count = keys_now.shape[0]
        per_group = row_count // group_count
        grad_now = rounded_grad[level_index].reshape(head_count, group_count, per_group, keys_now.shape[1])
        weight_now = rounded[level_index].reshape(head_count, group_count, per_group, keys_now.shape[1])
        query_groups = query_f.reshape(group_count, per_group, head_count, head_width)
        grad_groups = grad_f.reshape(group_count, per_group, head_count, head_width)
        query_sum = query_sum + jnp.einsum('hgqk,gkhd->gqhd', grad_now, keys_now.astype(jnp.float32)).reshape(row_count, head_count, head_width)
        key_grads.append(inv_root * jnp.einsum('hgqk,gqhd->gkhd', grad_now, query_groups))
        value_grads.append(jnp.einsum('hgqk,gqhd->gkhd', weight_now, grad_groups))
    return (attn_sum.astype(jnp.bfloat16), (inv_root * query_sum).astype(jnp.bfloat16), key_grads, value_grads)

def head_pass(pieces):
    queries, key_vectors, value_vectors, grad_attn, slopes = pieces
    key_levels = [key_vectors]
    value_levels = [value_vectors]
    for level_id in range(1, LEVELS):
        key_levels.append(pool_pairs(key_levels[-1]))
        value_levels.append(pool_pairs(value_levels[-1]))
    groups_k = [key_vectors.reshape(TOKENS // B, B, 1, HEAD_DIM)]
    groups_v = [value_vectors.reshape(TOKENS // B, B, 1, HEAD_DIM)]
    biases = [jnp.zeros((1,), jnp.float32)]
    for level_id in range(LEVELS):
        group_count = TOKENS // (B * 2 ** level_id)
        groups_k.append(swap_pairs(key_levels[level_id].reshape(group_count, B, 1, HEAD_DIM)))
        groups_v.append(swap_pairs(value_levels[level_id].reshape(group_count, B, 1, HEAD_DIM)))
        biases.append(level_id * LOG_TWO - slopes * (level_id + 1.0))
    attn, grad_q, key_grads, value_grads = attend(queries, groups_k, groups_v, biases, grad_attn)
    carry_k = swap_pairs(key_grads[LEVELS]).reshape(-1, 1, HEAD_DIM)
    carry_v = swap_pairs(value_grads[LEVELS]).reshape(-1, 1, HEAD_DIM)
    for level_id in reversed(range(LEVELS - 1)):
        carry_k = swap_pairs(key_grads[level_id + 1]).reshape(-1, 1, HEAD_DIM) + unpool_pairs(carry_k)
        carry_v = swap_pairs(value_grads[level_id + 1]).reshape(-1, 1, HEAD_DIM) + unpool_pairs(carry_v)
    grad_k = (carry_k + key_grads[0].reshape(-1, 1, HEAD_DIM)).astype(jnp.bfloat16)
    grad_v = (carry_v + value_grads[0].reshape(-1, 1, HEAD_DIM)).astype(jnp.bfloat16)
    return (attn, grad_q, grad_k, grad_v)

def split_heads(matrix):
    return matrix.reshape(TOKENS, HEADS, HEAD_DIM).transpose(1, 0, 2)[:, :, None, :]

def merge_heads(stacked):
    return stacked[:, :, 0, :].transpose(1, 0, 2).reshape(TOKENS, D)

def reference(queries, key_vectors, value_vectors, slopes, w_out, grad_out):
    grad_attn = jnp.dot(grad_out, w_out.T, preferred_element_type=jnp.float32).astype(jnp.bfloat16)
    attn, grad_q, grad_k, grad_v = lax.map(head_pass, (split_heads(queries), split_heads(key_vectors), split_heads(value_vectors), split_heads(grad_attn), slopes[:, None]))
    layer_out = jnp.dot(merge_heads(attn), w_out, preferred_element_type=jnp.float32).astype(jnp.bfloat16)
    return (layer_out, merge_heads(grad_q), merge_heads(grad_k), merge_heads(grad_v))
```

```python
import functools
import math

import jax
import jax.numpy as jnp
from jax import lax
from jax.experimental import pallas as pl
from jax.experimental.pallas import tpu as pltpu
from jax.sharding import PartitionSpec as P

B = 128
HEAD = 128
HALF = 512
HEADS = 4
KEYS = 1024
LOG_TWO = math.log(2.0)
LOG2E = 1.0 / LOG_TWO
ROOT = 1.0 / math.sqrt(HEAD)
F32 = jnp.float32
BF16 = jnp.bfloat16
MESH = pl.DeviceIdType.MESH

L1, L2, L3, L4, L5, L6 = 256, 384, 512, 640, 768, 896


def flip(index, bits):
    out = index
    for bit in bits:
        side = (index // (1 << bit)) % 2
        out = out + (1 - 2 * side) * (1 << bit)
    return out


def bits_of(mask, first):
    return [first + i for i in range(3) if mask >> i & 1]


def dot(a, b, dims=((1,), (0,))):
    return lax.dot_general(a, b, (dims, ((), ())), preferred_element_type=F32)


def pool_matrix(rows):
    r = lax.broadcasted_iota(jnp.int32, (rows // 2, rows), 0)
    c = lax.broadcasted_iota(jnp.int32, (rows // 2, rows), 1)
    return jnp.where(c // 2 == r, 0.5, 0.0).astype(BF16)


def pool(x):
    return dot(pool_matrix(x.shape[0]), x).astype(BF16)


def spread_matrix(rows, parts):
    blocks = []
    for ratio, width, copies in parts:
        r = lax.broadcasted_iota(jnp.int32, (rows, width * copies), 0)
        c = lax.broadcasted_iota(jnp.int32, (rows, width * copies), 1)
        blocks.append(jnp.where(r // ratio == c % width, 1.0 / ratio, 0.0).astype(BF16))
    return blocks


def kernel(
    slopes, q, k, v, g, w_hbm,
    layer_out, grad_q, grad_k, grad_v,
    kv, qc, gc, gfar, w, s1, s2, s3, a4, a5, a6, scores, gradw, prob, dsc,
    out, out3, back, g4, zin, acc, attn, whole, ga, send_part, recv_part, peer_q, peer_kv,
    send_sem, recv_sem, w_sem,
):
    ctx = lax.axis_index("ctx")
    head = lax.axis_index("head")
    core = ctx % 2
    mine = pl.ds(pl.multiple_of(core * HALF, HALF), HALF)
    theirs = pl.ds(pl.multiple_of((1 - core) * HALF, HALF), HALF)
    my_cols = pl.ds(pl.multiple_of(head * 1024, 1024), 1024)
    far_cols = pl.ds(pl.multiple_of((1 - head) * 1024, 1024), 1024)

    other = (flip(ctx, [0]), head)
    across = (ctx, 1 - head)
    z_peer = [None] + [(flip(ctx, bits_of(m, 1)), head) for m in range(1, 8)]
    xy_peer = [None] + [(flip(ctx, bits_of(m, 4)), head) for m in range(1, 8)]

    barrier = pltpu.get_barrier_semaphore()
    peers = [other, across] + z_peer[1:] + xy_peer[1:]
    for peer in peers:
        pl.semaphore_signal(barrier, inc=1, device_id=peer, device_id_type=MESH)

    load_w = pltpu.make_async_copy(w_hbm, w, w_sem)
    load_w.start()
    kv[0:128, 0:HALF] = k[:, mine]
    kv[0:128, HALF:1024] = v[:, mine]
    qc[0:128, :] = q[:, mine]

    pl.semaphore_wait(barrier, len(peers))

    count = [0]
    started = []

    def send(src, dst, peer):
        slot = count[0]
        count[0] += 1
        copy = pltpu.make_async_remote_copy(
            src_ref=src, dst_ref=dst, send_sem=send_sem.at[slot], recv_sem=recv_sem.at[slot],
            device_id=peer, device_id_type=MESH,
        )
        copy.start()
        started.append(copy)
        return copy

    in_k = send(k.at[:, theirs], kv.at[128:256, 0:HALF], other)
    in_v = send(v.at[:, theirs], kv.at[128:256, HALF:1024], other)
    in_g = send(g, gfar, across)
    in_q = send(q.at[:, theirs], qc.at[128:256, :], other)

    in_k.wait_recv()
    in_v.wait_recv()
    s1[...] = pool(kv[0:256, :])
    s2[...] = pool(s1[...])
    s3[...] = pool(s2[...])
    a4[0:16, :] = pool(s3[...])
    in3 = [send(s3, kv.at[L3 + 32 * (m - 4):L3 + 32 * (m - 3), :], z_peer[m]) for m in range(4, 8)]
    in4 = [send(a4.at[0:16, :], a4.at[16 * m:16 * (m + 1), :], z_peer[m]) for m in range(1, 4)]
    in2 = [send(s2, kv.at[L2 + 64 * (m - 2):L2 + 64 * (m - 1), :], z_peer[m]) for m in range(2, 4)]
    in1 = send(s1, kv.at[L1:L2, :], z_peer[1])

    load_w.wait()
    in_g.wait_recv()
    ga[...] = (
        dot(g[...], w[:, my_cols], ((1,), (1,))) + dot(gfar[...], w[:, far_cols], ((1,), (1,)))
    ).astype(BF16)
    gc[0:128, :] = ga[:, mine]
    in_ga = send(ga.at[:, theirs], gc.at[128:256, :], other)

    for copy in in3 + in4:
        copy.wait_recv()
    a4[64:128, :] = pool(kv[L3:L4, :])
    a5[...] = pool(a4[...])
    a6[...] = pool(a5[...])
    far4 = [send(a4, kv.at[L4:L5, :], xy_peer[1])]
    far5 = [send(a5, kv.at[L5 + 64 * (m - 2):L5 + 64 * (m - 1), :], xy_peer[m]) for m in range(2, 4)]
    far6 = [send(a6, kv.at[L6 + 32 * (m - 4):L6 + 32 * (m - 3), :], xy_peer[m]) for m in range(4, 8)]

    in_q.wait_recv()
    in_ga.wait_recv()

    def level_bias(h, level):
        slope = slopes[core * HEADS + h]
        return (level * LOG_TWO - slope * (level + 1.0)) * LOG2E

    def score_rows(h, low, high, bias):
        rows = slice(low, high)
        lanes = slice(h * HEAD, (h + 1) * HEAD)
        s = dot(kv[rows, lanes], qc[:, lanes], ((1,), (1,))) * (ROOT * LOG2E) + bias
        scores[h, rows, :] = s
        gradw[h, rows, :] = dot(
            kv[rows, HALF + h * HEAD:HALF + (h + 1) * HEAD], gc[:, lanes], ((1,), (1,))
        )
        return jnp.max(s, axis=0, keepdims=True)

    tops = []
    for h in range(HEADS):
        lane = lax.broadcasted_iota(jnp.int32, (1, 256), 1)
        bias = level_bias(h, 0)
        top = score_rows(h, 0, 128, jnp.where(lane < 128, 0.0, bias))
        top = jnp.maximum(top, score_rows(h, 128, 256, jnp.where(lane < 128, bias, 0.0)))
        tops.append(top)
    for level, low, copies in ((3, L3, []), (2, L2, in2), (1, L1, [in1])):
        for copy in copies:
            copy.wait_recv()
        for h in range(HEADS):
            tops[h] = jnp.maximum(tops[h], score_rows(h, low, low + 128, level_bias(h, level)))
    for level, low, copies in ((4, L4, far4), (5, L5, far5), (6, L6, far6)):
        for copy in copies:
            copy.wait_recv()
        for h in range(HEADS):
            tops[h] = jnp.maximum(tops[h], score_rows(h, low, low + 128, level_bias(h, level)))

    def gradients(h, low, high):
        lanes = slice(h * HEAD, (h + 1) * HEAD)
        d_key = dot(dsc[h, low:high, :], qc[:, lanes]) * ROOT
        d_value = dot(prob[h, low:high, :], gc[:, lanes])
        return d_key, d_value

    for h in range(HEADS):
        total = jnp.zeros((1, 256), F32)
        center = jnp.zeros((1, 256), F32)
        for low in range(0, KEYS, 128):
            e = jnp.exp2(scores[h, low:low + 128, :] - tops[h])
            scores[h, low:low + 128, :] = e
            total = total + jnp.sum(e, axis=0, keepdims=True)
            center = center + jnp.sum(e * gradw[h, low:low + 128, :], axis=0, keepdims=True)
        scale = 1.0 / total
        center = center * scale
        for low in range(0, KEYS, 128):
            weight = scores[h, low:low + 128, :] * scale
            prob[h, low:low + 128, :] = weight.astype(BF16)
            dsc[h, low:low + 128, :] = (weight * (gradw[h, low:low + 128, :] - center)).astype(BF16)
        d_key, d_value = gradients(h, L4, KEYS)
        out[L4 - 256:KEYS - 256, h * HEAD:(h + 1) * HEAD] = d_key.astype(BF16)
        out[L4 - 256:KEYS - 256, HALF + h * HEAD:HALF + (h + 1) * HEAD] = d_value.astype(BF16)

    def piece(low, rows):
        return out.at[low - 256:low - 256 + rows, :]

    back4 = [send(piece(L4, 128), back.at[0:128, :], xy_peer[1])]
    back4 += [
        send(piece(L5 + 64 * (m - 2), 64), back.at[128 + 64 * (m - 2):128 + 64 * (m - 1), :], xy_peer[m])
        for m in range(2, 4)
    ]
    back4 += [
        send(piece(L6 + 32 * (m - 4), 32), back.at[256 + 32 * (m - 4):256 + 32 * (m - 3), :], xy_peer[m])
        for m in range(4, 8)
    ]

    for h in range(HEADS):
        d_key, d_value = gradients(h, L1, L3)
        out[0:256, h * HEAD:(h + 1) * HEAD] = d_key.astype(BF16)
        out[0:256, HALF + h * HEAD:HALF + (h + 1) * HEAD] = d_value.astype(BF16)
    home = [
        send(piece(L2 + 64 * (m - 2), 64), zin.at[128 + 64 * (m - 2):128 + 64 * (m - 1), :], z_peer[m])
        for m in range(2, 4)
    ]
    home += [send(piece(L1, 128), zin.at[0:128, :], z_peer[1])]

    for h in range(HEADS):
        lanes = slice(h * HEAD, (h + 1) * HEAD)
        attn_t = dot(kv[:, HALF + h * HEAD:HALF + (h + 1) * HEAD], prob[h], ((0,), (0,)))
        both = attn_t.T.astype(BF16)
        whole[:, pl.ds(pl.multiple_of(core * HALF + h * HEAD, HEAD), HEAD)] = both[0:128]
        attn[:, lanes] = both[128:256]
    return_attn = send(attn, whole.at[:, mine], other)

    for h in range(HEADS):
        lanes = slice(h * HEAD, (h + 1) * HEAD)
        dq_t = dot(kv[:, lanes], dsc[h], ((0,), (0,))) * ROOT
        both = dq_t.T.astype(BF16)
        grad_q[:, pl.ds(pl.multiple_of(core * HALF + h * HEAD, HEAD), HEAD)] = both[0:128]
        peer_q[:, lanes] = both[128:256]
    return_q = send(peer_q, grad_q.at[:, mine], other)

    return_attn.wait_recv()
    send_part[...] = dot(whole[...], w[:, far_cols]).astype(BF16)
    part = send(send_part, recv_part, across)

    for h in range(HEADS):
        d_key, d_value = gradients(h, L3, L4)
        out3[:, h * HEAD:(h + 1) * HEAD] = d_key
        out3[:, HALF + h * HEAD:HALF + (h + 1) * HEAD] = d_value
        d_key, d_value = gradients(h, 0, 256)
        acc[:, h * HEAD:(h + 1) * HEAD] = d_key
        acc[:, HALF + h * HEAD:HALF + (h + 1) * HEAD] = d_value

    for copy in back4:
        copy.wait_recv()
    mix = spread_matrix(128, ((1, 128, 1), (2, 64, 2), (4, 32, 4)))
    folded = sum(dot(mix[i], back[128 * i:128 * (i + 1), :]) for i in range(3))
    g4[...] = folded.astype(BF16)
    zin[384:400, :] = g4[0:16, :]
    unpool = spread_matrix(128, ((2, 64, 1),))[0]
    out[L3 - 256:L4 - 256, :] = (out3[...] + dot(unpool, g4[64:128, :])).astype(BF16)
    home += [
        send(piece(L3 + 32 * (m - 4), 32), zin.at[256 + 32 * (m - 4):256 + 32 * (m - 3), :], z_peer[m])
        for m in range(4, 8)
    ]
    home += [
        send(g4.at[16 * m:16 * (m + 1), :], zin.at[384 + 16 * m:384 + 16 * (m + 1), :], z_peer[m])
        for m in range(1, 4)
    ]

    own_part = dot(whole[...], w[:, my_cols])
    part.wait_recv()
    layer_out[...] = (own_part + recv_part[...].astype(F32)).astype(BF16)

    for copy in home:
        copy.wait_recv()
    mix = spread_matrix(256, ((2, 128, 1), (4, 64, 2), (8, 32, 4), (16, 16, 4)))
    final = acc[...]
    for i in range(4):
        rows = slice(128 * i, min(128 * (i + 1), 448))
        final = final + dot(mix[i], zin[rows, :])
    done = final.astype(BF16)
    peer_kv[...] = done[128:256, :]
    return_k = send(peer_kv.at[:, 0:HALF], grad_k.at[:, mine], other)
    return_v = send(peer_kv.at[:, HALF:1024], grad_v.at[:, mine], other)
    grad_k[:, mine] = done[0:128, 0:HALF]
    grad_v[:, mine] = done[0:128, HALF:1024]
    return_q.wait_recv()
    return_k.wait_recv()
    return_v.wait_recv()
    for copy in started:
        copy.wait_send()


COPIES = 8 + 2 + 2 * (10 + 7)


def local(queries, key_vectors, value_vectors, slopes, w_out, grad_out):
    block = jax.ShapeDtypeStruct((B, 1024), BF16)
    vmem = pl.BlockSpec(memory_space=pltpu.VMEM)
    return pl.pallas_call(
        kernel,
        out_shape=[block] * 4,
        in_specs=[pl.BlockSpec(memory_space=pltpu.SMEM)] + [vmem] * 4 + [pl.BlockSpec(memory_space=pl.ANY)],
        out_specs=[vmem] * 4,
        scratch_shapes=[
            pltpu.VMEM((KEYS, 1024), BF16),
            pltpu.VMEM((256, HALF), BF16),
            pltpu.VMEM((256, HALF), BF16),
            pltpu.VMEM((128, 1024), BF16),
            pltpu.VMEM((1024, 2048), BF16),
            pltpu.VMEM((128, 1024), BF16),
            pltpu.VMEM((64, 1024), BF16),
            pltpu.VMEM((32, 1024), BF16),
            pltpu.VMEM((128, 1024), BF16),
            pltpu.VMEM((64, 1024), BF16),
            pltpu.VMEM((32, 1024), BF16),
            pltpu.VMEM((HEADS, KEYS, 256), F32),
            pltpu.VMEM((HEADS, KEYS, 256), F32),
            pltpu.VMEM((HEADS, KEYS, 256), BF16),
            pltpu.VMEM((HEADS, KEYS, 256), BF16),
            pltpu.VMEM((768, 1024), BF16),
            pltpu.VMEM((128, 1024), F32),
            pltpu.VMEM((384, 1024), BF16),
            pltpu.VMEM((128, 1024), BF16),
            pltpu.VMEM((448, 1024), BF16),
            pltpu.VMEM((256, 1024), F32),
            pltpu.VMEM((128, HALF), BF16),
            pltpu.VMEM((128, 1024), BF16),
            pltpu.VMEM((128, 1024), BF16),
            pltpu.VMEM((128, 1024), BF16),
            pltpu.VMEM((128, 1024), BF16),
            pltpu.VMEM((128, HALF), BF16),
            pltpu.VMEM((128, 1024), BF16),
            pltpu.SemaphoreType.DMA((COPIES,)),
            pltpu.SemaphoreType.DMA((COPIES,)),
            pltpu.SemaphoreType.DMA,
        ],
        compiler_params=pltpu.CompilerParams(
            collective_id=0, has_side_effects=True, vmem_limit_bytes=50 * 1024 * 1024
        ),
        cost_estimate=pl.CostEstimate(flops=2_700_000_000, bytes_accessed=8_000_000, transcendentals=1_000_000),
    )(slopes, queries, key_vectors, value_vectors, grad_out, w_out)


def solution(mesh):
    cut = P("ctx", "head")
    return jax.shard_map(
        local,
        mesh=mesh,
        in_specs=(cut, cut, cut, P("head"), P("head", None), cut),
        out_specs=(cut, cut, cut, cut),
        check_vma=False,
    )
```

```python
import math

import jax
import jax.numpy as jnp
from jax import lax
from jax.experimental import pallas as pl
from jax.experimental.pallas import tpu as pltpu
from jax.sharding import PartitionSpec as P

B = 128
HEAD = 128
HALF = 512
HEADS = 4
KEYS = 1024
LOG_TWO = math.log(2.0)
LOG2E = 1.0 / LOG_TWO
ROOT = 1.0 / math.sqrt(HEAD)
F32 = jnp.float32
BF16 = jnp.bfloat16
MESH = pl.DeviceIdType.MESH

L1, L2, L3, L4, L5, L6 = 256, 384, 512, 640, 768, 896


def flip(index, bits):
    out = index
    for bit in bits:
        side = (index // (1 << bit)) % 2
        out = out + (1 - 2 * side) * (1 << bit)
    return out


def bits_of(mask, first):
    return [first + i for i in range(3) if mask >> i & 1]


def dot(a, b, dims=((1,), (0,))):
    return lax.dot_general(a, b, (dims, ((), ())), preferred_element_type=F32)


def grid_of(rows, columns):
    r = lax.broadcasted_iota(jnp.int32, (rows, columns), 0)
    c = lax.broadcasted_iota(jnp.int32, (rows, columns), 1)
    return r, c


def pool_f32(x):
    r, c = grid_of(x.shape[0] // 2, x.shape[0])
    return dot(jnp.where(c // 2 == r, 0.5, 0.0).astype(BF16), x)


def pool(x):
    return pool_f32(x).astype(BF16)


def spread(rows, parts):
    blocks = []
    for ratio, width, copies in parts:
        r, c = grid_of(rows, width * copies)
        blocks.append(jnp.where(r // ratio == c % width, 1.0 / ratio, 0.0).astype(BF16))
    return jnp.concatenate(blocks, axis=1)


def pack(x):
    return jnp.concatenate([x[:, 0:HALF], x[:, HALF:1024]], axis=0).astype(BF16)


def kernel(
    slopes_in, q, k, v, g, w_in,
    layer_out, grad_q, grad_k, grad_v,
    slopes, kv, kt, qc, gc, gown, gfar, w, s1, s2, s3, s4, packed, a4, a5, a6,
    scores, gradw, prob, dsc, out, out3, back, n4, zin, zin4, acc, acc_in,
    attn, whole, ga, send_part, recv_part, peer_q,
    send_sem, recv_sem, local_sem,
):
    ctx = lax.axis_index("ctx")
    head = lax.axis_index("head")
    core = ctx % 2
    mine = pl.ds(pl.multiple_of(core * HALF, HALF), HALF)
    theirs = pl.ds(pl.multiple_of((1 - core) * HALF, HALF), HALF)
    my_cols = pl.ds(pl.multiple_of(head * 1024, 1024), 1024)
    far_cols = pl.ds(pl.multiple_of((1 - head) * 1024, 1024), 1024)

    other = (flip(ctx, [0]), head)
    across = (ctx, 1 - head)
    z_peer = [[(flip(ctx, [0] * sub + bits_of(m, 1)), head) for sub in range(2)] for m in range(8)]
    xy_peer = [None] + [(flip(ctx, bits_of(m, 4)), head) for m in range(1, 8)]

    barrier = pltpu.get_barrier_semaphore()
    peers = [other, across] + sum(z_peer[1:], []) + xy_peer[1:]
    for peer in peers:
        pl.semaphore_signal(barrier, inc=1, device_id=peer, device_id_type=MESH)

    def load(src, dst, slot):
        copy = pltpu.make_async_copy(src, dst, local_sem.at[slot])
        copy.start()
        return copy

    load_kv = [
        load(k.at[:, mine], kv.at[0:128, 0:HALF], 0),
        load(v.at[:, mine], kv.at[0:128, HALF:1024], 1),
        load(k.at[:, theirs], kt.at[:, 0:HALF], 2),
        load(v.at[:, theirs], kt.at[:, HALF:1024], 3),
    ]
    load_rest = [
        load(q.at[:, mine], qc.at[0:128, :], 4),
        load(g, gown, 5),
        load(slopes_in, slopes, 6),
        load(w_in, w, 7),
    ]

    for copy in load_kv:
        copy.wait()
    for j, rows in ((0, kv[0:128, :]), (1, kt[...])):
        s1[j] = pool(rows)
        s2[j] = pool(s1[j])
        s3[j] = pool(s2[j])
        s4[j] = pack(pool_f32(s3[j]))
    packed[0:16, :] = s4[0]

    pl.semaphore_wait(barrier, len(peers))

    count = [0]
    started = []

    def send(src, dst, peer):
        slot = count[0]
        count[0] += 1
        copy = pltpu.make_async_remote_copy(
            src_ref=src, dst_ref=dst, send_sem=send_sem.at[slot], recv_sem=recv_sem.at[slot],
            device_id=peer, device_id_type=MESH,
        )
        copy.start()
        started.append(copy)
        return copy

    def packed_at(m, sub):
        return packed.at[32 * m + 16 * sub:32 * m + 16 * sub + 16, :]

    in4 = [send(s4.at[1], packed_at(0, 1), other)]
    in4 += [send(s4.at[sub], packed_at(m, sub), z_peer[m][sub]) for m in range(1, 4) for sub in range(2)]

    def z_sends(source, low, rows, masks):
        return [
            send(
                source.at[sub],
                kv.at[low + (2 * i + sub) * rows:low + (2 * i + sub + 1) * rows, :],
                z_peer[m][sub],
            )
            for i, m in enumerate(masks)
            for sub in range(2)
        ]

    in3 = z_sends(s3, L3, 16, (4, 5, 6, 7))
    in_kv = send(kt, kv.at[128:256, :], other)
    in_q = send(q.at[:, theirs], qc.at[128:256, :], other)
    in_g = send(g, gfar, across)
    in2 = z_sends(s2, L2, 32, (2, 3))
    in1 = z_sends(s1, L1, 64, (1,))

    def xy_sends(half):
        copies = [send(a4.at[64 * half:64 * half + 64, :], kv.at[L4 + 64 * half:L4 + 64 * half + 64, :], xy_peer[1])]
        for m in range(2, 4):
            low = L5 + 64 * (m - 2) + 32 * half
            copies.append(send(a5.at[32 * half:32 * half + 32, :], kv.at[low:low + 32, :], xy_peer[m]))
        for m in range(4, 8):
            low = L6 + 32 * (m - 4) + 16 * half
            copies.append(send(a6.at[16 * half:16 * half + 16, :], kv.at[low:low + 16, :], xy_peer[m]))
        return copies

    for copy in in4:
        copy.wait_recv()
    r, c = grid_of(64, 128)
    at_k = (r // 8) * 16 + r % 8
    a4[0:64, 0:HALF] = dot(jnp.where(c == at_k, 1.0, 0.0).astype(BF16), packed[...]).astype(BF16)
    a4[0:64, HALF:1024] = dot(jnp.where(c == at_k + 8, 1.0, 0.0).astype(BF16), packed[...]).astype(BF16)
    a5[0:32, :] = pool(a4[0:64, :])
    a6[0:16, :] = pool(a5[0:32, :])
    far = xy_sends(0)

    for copy in load_rest:
        copy.wait()
    in_g.wait_recv()
    ga[...] = (
        dot(gown[...], w[:, my_cols], ((1,), (1,))) + dot(gfar[...], w[:, far_cols], ((1,), (1,)))
    ).astype(BF16)
    gc[0:128, :] = ga[:, mine]
    in_ga = send(ga.at[:, theirs], gc.at[128:256, :], other)

    for copy in in3:
        copy.wait_recv()
    a4[64:128, :] = pool(kv[L3:L4, :])
    a5[32:64, :] = pool(a4[64:128, :])
    a6[16:32, :] = pool(a5[32:64, :])
    far += xy_sends(1)

    in_kv.wait_recv()
    in_q.wait_recv()
    in_ga.wait_recv()

    def level_bias(h, level):
        slope = slopes[core * HEADS + h]
        return (level * LOG_TWO - slope * (level + 1.0)) * LOG2E

    def score_rows(h, low, high, bias):
        rows = slice(low, high)
        lanes = slice(h * HEAD, (h + 1) * HEAD)
        s = dot(kv[rows, lanes], qc[:, lanes], ((1,), (1,))) * (ROOT * LOG2E) + bias
        scores[h, rows, :] = s
        gradw[h, rows, :] = dot(
            kv[rows, HALF + h * HEAD:HALF + (h + 1) * HEAD], gc[:, lanes], ((1,), (1,))
        )
        return jnp.max(s, axis=0, keepdims=True)

    tops = []
    for h in range(HEADS):
        lane = lax.broadcasted_iota(jnp.int32, (1, 256), 1)
        bias = level_bias(h, 0)
        top = score_rows(h, 0, 128, jnp.where(lane < 128, 0.0, bias))
        top = jnp.maximum(top, score_rows(h, 128, 256, jnp.where(lane < 128, bias, 0.0)))
        tops.append(top)
    for level, low, copies in ((3, L3, []), (2, L2, in2), (1, L1, in1), (4, L4, far), (5, L5, []), (6, L6, [])):
        for copy in copies:
            copy.wait_recv()
        for h in range(HEADS):
            tops[h] = jnp.maximum(tops[h], score_rows(h, low, low + 128, level_bias(h, level)))

    def gradients(h, low, high):
        lanes = slice(h * HEAD, (h + 1) * HEAD)
        d_key = dot(dsc[h, low:high, :], qc[:, lanes]) * ROOT
        d_value = dot(prob[h, low:high, :], gc[:, lanes])
        return d_key, d_value

    for h in range(HEADS):
        total = jnp.zeros((1, 256), F32)
        center = jnp.zeros((1, 256), F32)
        for low in range(0, KEYS, 128):
            e = jnp.exp2(scores[h, low:low + 128, :] - tops[h])
            scores[h, low:low + 128, :] = e
            total = total + jnp.sum(e, axis=0, keepdims=True)
            center = center + jnp.sum(e * gradw[h, low:low + 128, :], axis=0, keepdims=True)
        scale = 1.0 / total
        center = center * scale
        for low in range(0, KEYS, 128):
            weight = scores[h, low:low + 128, :] * scale
            prob[h, low:low + 128, :] = weight.astype(BF16)
            dsc[h, low:low + 128, :] = (weight * (gradw[h, low:low + 128, :] - center)).astype(BF16)
        d_key, d_value = gradients(h, L4, KEYS)
        out[L4 - 256:KEYS - 256, h * HEAD:(h + 1) * HEAD] = d_key.astype(BF16)
        out[L4 - 256:KEYS - 256, HALF + h * HEAD:HALF + (h + 1) * HEAD] = d_value.astype(BF16)

    def piece(low, rows):
        return out.at[low - 256:low - 256 + rows, :]

    def xy_back(half):
        copies = [send(piece(L4 + 64 * half, 64), back.at[half, 0:64, :], xy_peer[1])]
        for m in range(2, 4):
            at = 64 + 32 * (m - 2)
            copies.append(send(piece(L5 + 64 * (m - 2) + 32 * half, 32), back.at[half, at:at + 32, :], xy_peer[m]))
        for m in range(4, 8):
            at = 128 + 16 * (m - 4)
            copies.append(send(piece(L6 + 32 * (m - 4) + 16 * half, 16), back.at[half, at:at + 16, :], xy_peer[m]))
        return copies

    back_far = xy_back(1)
    back_near = xy_back(0)

    for h in range(HEADS):
        d_key, d_value = gradients(h, L1, L3)
        out[0:256, h * HEAD:(h + 1) * HEAD] = d_key.astype(BF16)
        out[0:256, HALF + h * HEAD:HALF + (h + 1) * HEAD] = d_value.astype(BF16)

    def z_back(low, rows, masks, at):
        return [
            send(
                piece(low + (2 * i + sub) * rows, rows),
                zin.at[sub, at + i * rows:at + (i + 1) * rows, :],
                z_peer[m][sub],
            )
            for i, m in enumerate(masks)
            for sub in range(2)
        ]

    home = z_back(L2, 32, (2, 3), 64) + z_back(L1, 64, (1,), 0)

    for h in range(HEADS):
        lanes = slice(h * HEAD, (h + 1) * HEAD)
        attn_t = dot(kv[:, HALF + h * HEAD:HALF + (h + 1) * HEAD], prob[h], ((0,), (0,)))
        both = attn_t.T.astype(BF16)
        whole[:, pl.ds(pl.multiple_of(core * HALF + h * HEAD, HEAD), HEAD)] = both[0:128]
        attn[:, lanes] = both[128:256]
    return_attn = send(attn, whole.at[:, mine], other)

    for h in range(HEADS):
        d_key, d_value = gradients(h, L3, L4)
        out3[:, h * HEAD:(h + 1) * HEAD] = d_key
        out3[:, HALF + h * HEAD:HALF + (h + 1) * HEAD] = d_value

    return_attn.wait_recv()
    send_part[...] = dot(whole[...], w[:, far_cols]).astype(BF16)
    part = send(send_part, recv_part, across)

    for copy in back_far:
        copy.wait_recv()
    mix = spread(128, ((2, 64, 1), (4, 32, 2), (8, 16, 4)))
    out[L3 - 256:L4 - 256, :] = (out3[...] + dot(mix, back[1])).astype(BF16)
    home += z_back(L3, 16, (4, 5, 6, 7), 128)

    for copy in back_near:
        copy.wait_recv()
    g4 = dot(spread(64, ((1, 64, 1), (2, 32, 2), (4, 16, 4))), back[0])
    for m in range(4):
        for sub in range(2):
            at = 16 * m + 8 * sub
            n4[2 * m + sub] = pack(g4[at:at + 8])
    zin4[0, 0:16, :] = n4[0]
    home += [send(n4.at[1], zin4.at[1, 0:16, :], other)]
    home += [
        send(n4.at[2 * m + sub], zin4.at[sub, 16 * m:16 * m + 16, :], z_peer[m][sub])
        for m in range(1, 4)
        for sub in range(2)
    ]

    for h in range(HEADS):
        d_key, d_value = gradients(h, 0, 256)
        acc[:, h * HEAD:(h + 1) * HEAD] = d_key
        acc[:, HALF + h * HEAD:HALF + (h + 1) * HEAD] = d_value
    home += [send(acc.at[128:256, :], acc_in, other)]

    for h in range(HEADS):
        lanes = slice(h * HEAD, (h + 1) * HEAD)
        dq_t = dot(kv[:, lanes], dsc[h], ((0,), (0,))) * ROOT
        both = dq_t.T.astype(BF16)
        grad_q[:, pl.ds(pl.multiple_of(core * HALF + h * HEAD, HEAD), HEAD)] = both[0:128]
        peer_q[:, lanes] = both[128:256]
    home += [send(peer_q, grad_q.at[:, mine], other)]

    own_part = dot(whole[...], w[:, my_cols])
    part.wait_recv()
    layer_out[...] = (own_part + recv_part[...].astype(F32)).astype(BF16)

    r, c = grid_of(128, 64)
    low_k = jnp.where(c % 16 == r // 16, 1.0 / 16, 0.0).astype(BF16)
    low_v = jnp.where(c % 16 == r // 16 + 8, 1.0 / 16, 0.0).astype(BF16)
    for copy in home:
        copy.wait_recv()
    for sub, base, cols in ((0, acc, mine), (1, acc_in, theirs)):
        total = base[0:128, :] + dot(mix, zin[sub])
        grad_k[:, cols] = (total[:, 0:HALF] + dot(low_k, zin4[sub])).astype(BF16)
        grad_v[:, cols] = (total[:, HALF:1024] + dot(low_v, zin4[sub])).astype(BF16)
    for copy in started:
        copy.wait_send()


COPIES = 9 + 2 + 2 * (20 + 14)


def store(*refs):
    sems = refs[8]
    copies = [pltpu.make_async_copy(refs[i], refs[4 + i], sems.at[i]) for i in range(4)]
    for copy in copies:
        copy.start()
    for copy in copies:
        copy.wait()


def local(queries, key_vectors, value_vectors, slopes, w_out, grad_out):
    block = jax.ShapeDtypeStruct((B, 1024), BF16)
    vmem = pl.BlockSpec(memory_space=pltpu.VMEM)
    anywhere = pl.BlockSpec(memory_space=pl.ANY)
    results = pl.pallas_call(
        kernel,
        out_shape=[block] * 4,
        in_specs=[pl.BlockSpec(memory_space=pltpu.HBM)] * 6,
        out_specs=[vmem] * 4,
        scratch_shapes=[
            pltpu.SMEM((8,), F32),
            pltpu.VMEM((KEYS, 1024), BF16),
            pltpu.VMEM((128, 1024), BF16),
            pltpu.VMEM((256, HALF), BF16),
            pltpu.VMEM((256, HALF), BF16),
            pltpu.VMEM((128, 1024), BF16),
            pltpu.VMEM((128, 1024), BF16),
            pltpu.VMEM((1024, 2048), BF16),
            pltpu.VMEM((2, 64, 1024), BF16),
            pltpu.VMEM((2, 32, 1024), BF16),
            pltpu.VMEM((2, 16, 1024), BF16),
            pltpu.VMEM((2, 16, HALF), BF16),
            pltpu.VMEM((128, HALF), BF16),
            pltpu.VMEM((128, 1024), BF16),
            pltpu.VMEM((64, 1024), BF16),
            pltpu.VMEM((32, 1024), BF16),
            pltpu.VMEM((HEADS, KEYS, 256), F32),
            pltpu.VMEM((HEADS, KEYS, 256), F32),
            pltpu.VMEM((HEADS, KEYS, 256), BF16),
            pltpu.VMEM((HEADS, KEYS, 256), BF16),
            pltpu.VMEM((768, 1024), BF16),
            pltpu.VMEM((128, 1024), F32),
            pltpu.VMEM((2, 192, 1024), BF16),
            pltpu.VMEM((8, 16, HALF), BF16),
            pltpu.VMEM((2, 192, 1024), BF16),
            pltpu.VMEM((2, 64, HALF), BF16),
            pltpu.VMEM((256, 1024), F32),
            pltpu.VMEM((128, 1024), F32),
            pltpu.VMEM((128, HALF), BF16),
            pltpu.VMEM((128, 1024), BF16),
            pltpu.VMEM((128, 1024), BF16),
            pltpu.VMEM((128, 1024), BF16),
            pltpu.VMEM((128, 1024), BF16),
            pltpu.VMEM((128, HALF), BF16),
            pltpu.SemaphoreType.DMA((COPIES,)),
            pltpu.SemaphoreType.DMA((COPIES,)),
            pltpu.SemaphoreType.DMA((8,)),
        ],
        compiler_params=pltpu.CompilerParams(
            collective_id=0, has_side_effects=True, vmem_limit_bytes=63 * 1024 * 1024
        ),
        cost_estimate=pl.CostEstimate(flops=2_700_000_000, bytes_accessed=8_000_000, transcendentals=1_000_000),
    )(slopes, queries, key_vectors, value_vectors, grad_out, w_out)
    return pl.pallas_call(
        store,
        out_shape=[block] * 4,
        in_specs=[vmem] * 4,
        out_specs=[pl.BlockSpec(memory_space=pltpu.HBM)] * 4,
        scratch_shapes=[pltpu.SemaphoreType.DMA((4,))],
    )(*results)


def solution(mesh):
    cut = P("ctx", "head")
    return jax.shard_map(
        local,
        mesh=mesh,
        in_specs=(cut, cut, cut, P("head"), P("head", None), cut),
        out_specs=(cut, cut, cut, cut),
        check_vma=False,
    )
```

```python
import functools
import math

import jax
import jax.numpy as jnp
from jax import lax
from jax.experimental import pallas as pl
from jax.experimental.pallas import tpu as pltpu
from jax.sharding import PartitionSpec as P

B = 128
HEAD = 128
HALF = 512
HEADS = 4
KEYS = 1024
LOG_TWO = math.log(2.0)
LOG2E = 1.0 / LOG_TWO
ROOT = 1.0 / math.sqrt(HEAD)
F32 = jnp.float32
BF16 = jnp.bfloat16
MESH = pl.DeviceIdType.MESH

L1, L2, L3, L4, L5, L6 = 256, 384, 512, 640, 768, 896


def flip(index, bits):
    out = index
    for bit in bits:
        side = (index // (1 << bit)) % 2
        out = out + (1 - 2 * side) * (1 << bit)
    return out


def bits_of(mask, first):
    return [first + i for i in range(3) if mask >> i & 1]


def dot(a, b, dims=((1,), (0,))):
    return lax.dot_general(a, b, (dims, ((), ())), preferred_element_type=F32)


def grid_of(rows, columns):
    r = lax.broadcasted_iota(jnp.int32, (rows, columns), 0)
    c = lax.broadcasted_iota(jnp.int32, (rows, columns), 1)
    return r, c


def pool_f32(x):
    r, c = grid_of(x.shape[0] // 2, x.shape[0])
    return dot(jnp.where(c // 2 == r, 0.5, 0.0).astype(BF16), x)


def pool(x):
    return pool_f32(x).astype(BF16)


def spread(rows, parts):
    blocks = []
    for ratio, width, copies in parts:
        r, c = grid_of(rows, width * copies)
        blocks.append(jnp.where(r // ratio == c % width, 1.0 / ratio, 0.0).astype(BF16))
    return jnp.concatenate(blocks, axis=1)


def pack(x):
    return jnp.concatenate([x[:, 0:HALF], x[:, HALF:1024]], axis=0).astype(BF16)


def kernel(
    slopes_in, q, k, v, g, w_in,
    layer_out, grad_q, grad_k, grad_v,
    slopes, kv, kt, qc, gc, gown, gfar, w, s1, s2, s3, s4, packed, a4, a5, a6,
    scores, gradw, prob, dsc, out, out3, back, n4, zin, zin4, acc, acc_in,
    attn, whole, ga, send_part, recv_part, peer_q,
    send_sem, recv_sem, local_sem,
):
    ctx = lax.axis_index("ctx")
    head = lax.axis_index("head")
    core = ctx % 2
    mine = pl.ds(pl.multiple_of(core * HALF, HALF), HALF)
    theirs = pl.ds(pl.multiple_of((1 - core) * HALF, HALF), HALF)
    my_cols = pl.ds(pl.multiple_of(head * 1024, 1024), 1024)
    far_cols = pl.ds(pl.multiple_of((1 - head) * 1024, 1024), 1024)

    other = (flip(ctx, [0]), head)
    across = (ctx, 1 - head)
    z_peer = [[(flip(ctx, [0] * sub + bits_of(m, 1)), head) for sub in range(2)] for m in range(8)]
    xy_peer = [None] + [(flip(ctx, bits_of(m, 4)), head) for m in range(1, 8)]

    barrier = pltpu.get_barrier_semaphore()
    peers = [other, across] + sum(z_peer[1:], []) + xy_peer[1:]
    for peer in peers:
        pl.semaphore_signal(barrier, inc=1, device_id=peer, device_id_type=MESH)

    def load(src, dst, slot):
        copy = pltpu.make_async_copy(src, dst, local_sem.at[slot])
        copy.start()
        return copy

    load_kv = [
        load(k.at[:, mine], kv.at[0:128, 0:HALF], 0),
        load(v.at[:, mine], kv.at[0:128, HALF:1024], 1),
        load(k.at[:, theirs], kt.at[:, 0:HALF], 2),
        load(v.at[:, theirs], kt.at[:, HALF:1024], 3),
    ]
    load_rest = [
        load(q.at[:, mine], qc.at[0:128, :], 4),
        load(g, gown, 5),
        load(slopes_in, slopes, 6),
    ]

    for copy in load_kv:
        copy.wait()
    for j, rows in ((0, kv[0:128, :]), (1, kt[...])):
        s1[j] = pool(rows)
        s2[j] = pool(s1[j])
        s3[j] = pool(s2[j])
        s4[j] = pack(pool_f32(s3[j]))
    load_rest.append(load(w_in, w, 7))
    packed[0:16, :] = s4[0]

    pl.semaphore_wait(barrier, len(peers))

    count = [0]
    started = []

    def send(src, dst, peer):
        slot = count[0]
        count[0] += 1
        copy = pltpu.make_async_remote_copy(
            src_ref=src, dst_ref=dst, send_sem=send_sem.at[slot], recv_sem=recv_sem.at[slot],
            device_id=peer, device_id_type=MESH,
        )
        copy.start()
        started.append(copy)
        return copy

    def packed_at(m, sub):
        return packed.at[32 * m + 16 * sub:32 * m + 16 * sub + 16, :]

    in4 = [send(s4.at[1], packed_at(0, 1), other)]
    in4 += [send(s4.at[sub], packed_at(m, sub), z_peer[m][sub]) for m in range(1, 4) for sub in range(2)]

    def z_sends(source, low, rows, masks):
        return [
            send(
                source.at[sub],
                kv.at[low + (2 * i + sub) * rows:low + (2 * i + sub + 1) * rows, :],
                z_peer[m][sub],
            )
            for i, m in enumerate(masks)
            for sub in range(2)
        ]

    in3 = z_sends(s3, L3, 16, (4, 5, 6, 7))
    in_kv = send(kt, kv.at[128:256, :], other)
    in_q = send(q.at[:, theirs], qc.at[128:256, :], other)
    in_g = send(g, gfar, across)
    in2 = z_sends(s2, L2, 32, (2, 3))
    in1 = z_sends(s1, L1, 64, (1,))

    def xy_sends(half):
        copies = [send(a4.at[64 * half:64 * half + 64, :], kv.at[L4 + 64 * half:L4 + 64 * half + 64, :], xy_peer[1])]
        for m in range(2, 4):
            low = L5 + 64 * (m - 2) + 32 * half
            copies.append(send(a5.at[32 * half:32 * half + 32, :], kv.at[low:low + 32, :], xy_peer[m]))
        for m in range(4, 8):
            low = L6 + 32 * (m - 4) + 16 * half
            copies.append(send(a6.at[16 * half:16 * half + 16, :], kv.at[low:low + 16, :], xy_peer[m]))
        return copies

    for copy in in4:
        copy.wait_recv()
    r, c = grid_of(64, 128)
    at_k = (r // 8) * 16 + r % 8
    a4[0:64, 0:HALF] = dot(jnp.where(c == at_k, 1.0, 0.0).astype(BF16), packed[...]).astype(BF16)
    a4[0:64, HALF:1024] = dot(jnp.where(c == at_k + 8, 1.0, 0.0).astype(BF16), packed[...]).astype(BF16)
    a5[0:32, :] = pool(a4[0:64, :])
    a6[0:16, :] = pool(a5[0:32, :])
    far = xy_sends(0)

    for copy in load_rest:
        copy.wait()
    in_g.wait_recv()
    ga[...] = (
        dot(gown[...], w[:, my_cols], ((1,), (1,))) + dot(gfar[...], w[:, far_cols], ((1,), (1,)))
    ).astype(BF16)
    gc[0:128, :] = ga[:, mine]
    in_ga = send(ga.at[:, theirs], gc.at[128:256, :], other)

    for copy in in3:
        copy.wait_recv()
    a4[64:128, :] = pool(kv[L3:L4, :])
    a5[32:64, :] = pool(a4[64:128, :])
    a6[16:32, :] = pool(a5[32:64, :])
    far += xy_sends(1)

    in_kv.wait_recv()
    in_q.wait_recv()
    in_ga.wait_recv()

    def level_bias(h, level):
        slope = slopes[core * HEADS + h]
        return (level * LOG_TWO - slope * (level + 1.0)) * LOG2E

    def in_eights(x):
        return x.reshape(x.shape[0] // 8, 8, 256)

    def score_rows(h, low, bias):
        rows = slice(low, low + 128)
        lanes = slice(h * HEAD, (h + 1) * HEAD)
        s = dot(kv[rows, lanes], qc[:, lanes], ((1,), (1,))) * (ROOT * LOG2E) + bias
        scores[h, rows, :] = s
        gradw[h, rows, :] = dot(
            kv[rows, HALF + h * HEAD:HALF + (h + 1) * HEAD], gc[:, lanes], ((1,), (1,))
        )
        return jnp.max(in_eights(s), axis=0)

    lane = lax.broadcasted_iota(jnp.int32, (1, 256), 1)

    def bias_of(h, low):
        if low < L1:
            sibling = level_bias(h, 0)
            return jnp.where((lane < 128) == (low == 0), 0.0, sibling)
        return level_bias(h, {L1: 1, L2: 2, L3: 3, L4: 4, L5: 5, L6: 6}[low])

    def group(lows):
        stats = []
        for h in range(HEADS):
            top = functools.reduce(jnp.maximum, [score_rows(h, low, bias_of(h, low)) for low in lows])
            top = jnp.max(top, axis=0, keepdims=True)
            total = jnp.zeros((8, 256), F32)
            center = jnp.zeros((8, 256), F32)
            for low in lows:
                e = jnp.exp2(scores[h, low:low + 128, :] - top)
                scores[h, low:low + 128, :] = e
                total = total + jnp.sum(in_eights(e), axis=0)
                center = center + jnp.sum(in_eights(e * gradw[h, low:low + 128, :]), axis=0)
            stats.append((top, jnp.sum(total, axis=0, keepdims=True), jnp.sum(center, axis=0, keepdims=True)))
        return stats

    near_lows, mid_lows, far_lows = (0, 128, L3), (L2, L1), (L4, L5, L6)
    groups = [group(near_lows)]
    for copy in in2 + in1:
        copy.wait_recv()
    groups.append(group(mid_lows))
    for copy in far:
        copy.wait_recv()
    groups.append(group(far_lows))

    scales = []
    centers = []
    for h in range(HEADS):
        tops = [stats[h][0] for stats in groups]
        best = functools.reduce(jnp.maximum, tops)
        factors = [jnp.exp2(top - best) for top in tops]
        total = sum(f * stats[h][1] for f, stats in zip(factors, groups))
        center = sum(f * stats[h][2] for f, stats in zip(factors, groups))
        inverse = 1.0 / total
        scales.append([f * inverse for f in factors])
        centers.append(center * inverse)

    def normalise(h, index, lows):
        for low in lows:
            weight = scores[h, low:low + 128, :] * scales[h][index]
            prob[h, low:low + 128, :] = weight.astype(BF16)
            dsc[h, low:low + 128, :] = (weight * (gradw[h, low:low + 128, :] - centers[h])).astype(BF16)

    def gradients(h, low, high):
        lanes = slice(h * HEAD, (h + 1) * HEAD)
        d_key = dot(dsc[h, low:high, :], qc[:, lanes]) * ROOT
        d_value = dot(prob[h, low:high, :], gc[:, lanes])
        return d_key, d_value

    def put(h, low, high):
        d_key, d_value = gradients(h, low, high)
        out[low - 256:high - 256, h * HEAD:(h + 1) * HEAD] = d_key.astype(BF16)
        out[low - 256:high - 256, HALF + h * HEAD:HALF + (h + 1) * HEAD] = d_value.astype(BF16)

    for h in range(HEADS):
        normalise(h, 2, far_lows)
        put(h, L4, KEYS)

    def piece(low, rows):
        return out.at[low - 256:low - 256 + rows, :]

    def xy_back(half):
        copies = [send(piece(L4 + 64 * half, 64), back.at[half, 0:64, :], xy_peer[1])]
        for m in range(2, 4):
            at = 64 + 32 * (m - 2)
            copies.append(send(piece(L5 + 64 * (m - 2) + 32 * half, 32), back.at[half, at:at + 32, :], xy_peer[m]))
        for m in range(4, 8):
            at = 128 + 16 * (m - 4)
            copies.append(send(piece(L6 + 32 * (m - 4) + 16 * half, 16), back.at[half, at:at + 16, :], xy_peer[m]))
        return copies

    back_far = xy_back(1)
    back_near = xy_back(0)

    for h in range(HEADS):
        normalise(h, 1, mid_lows)
        put(h, L1, L3)

    def z_back(low, rows, masks, at):
        return [
            send(
                piece(low + (2 * i + sub) * rows, rows),
                zin.at[sub, at + i * rows:at + (i + 1) * rows, :],
                z_peer[m][sub],
            )
            for i, m in enumerate(masks)
            for sub in range(2)
        ]

    home = z_back(L2, 32, (2, 3), 64) + z_back(L1, 64, (1,), 0)

    for h in range(HEADS):
        normalise(h, 0, near_lows)
        lanes = slice(h * HEAD, (h + 1) * HEAD)
        attn_t = dot(kv[:, HALF + h * HEAD:HALF + (h + 1) * HEAD], prob[h], ((0,), (0,)))
        both = attn_t.T.astype(BF16)
        whole[:, pl.ds(pl.multiple_of(core * HALF + h * HEAD, HEAD), HEAD)] = both[0:128]
        attn[:, lanes] = both[128:256]
    return_attn = send(attn, whole.at[:, mine], other)

    for h in range(HEADS):
        d_key, d_value = gradients(h, L3, L4)
        out3[:, h * HEAD:(h + 1) * HEAD] = d_key
        out3[:, HALF + h * HEAD:HALF + (h + 1) * HEAD] = d_value

    return_attn.wait_recv()
    send_part[...] = dot(whole[...], w[:, far_cols]).astype(BF16)
    part = send(send_part, recv_part, across)

    for copy in back_far:
        copy.wait_recv()
    mix = spread(128, ((2, 64, 1), (4, 32, 2), (8, 16, 4)))
    out[L3 - 256:L4 - 256, :] = (out3[...] + dot(mix, back[1])).astype(BF16)
    home += z_back(L3, 16, (4, 5, 6, 7), 128)

    for copy in back_near:
        copy.wait_recv()
    g4 = dot(spread(64, ((1, 64, 1), (2, 32, 2), (4, 16, 4))), back[0])
    for m in range(4):
        for sub in range(2):
            at = 16 * m + 8 * sub
            n4[2 * m + sub] = pack(g4[at:at + 8])
    zin4[0, 0:16, :] = n4[0]
    home += [send(n4.at[1], zin4.at[1, 0:16, :], other)]
    home += [
        send(n4.at[2 * m + sub], zin4.at[sub, 16 * m:16 * m + 16, :], z_peer[m][sub])
        for m in range(1, 4)
        for sub in range(2)
    ]

    for h in range(HEADS):
        d_key, d_value = gradients(h, 0, 256)
        acc[:, h * HEAD:(h + 1) * HEAD] = d_key
        acc[:, HALF + h * HEAD:HALF + (h + 1) * HEAD] = d_value
    home += [send(acc.at[128:256, :], acc_in, other)]

    for h in range(HEADS):
        lanes = slice(h * HEAD, (h + 1) * HEAD)
        dq_t = dot(kv[:, lanes], dsc[h], ((0,), (0,))) * ROOT
        both = dq_t.T.astype(BF16)
        grad_q[:, pl.ds(pl.multiple_of(core * HALF + h * HEAD, HEAD), HEAD)] = both[0:128]
        peer_q[:, lanes] = both[128:256]
    home += [send(peer_q, grad_q.at[:, mine], other)]

    own_part = dot(whole[...], w[:, my_cols])
    part.wait_recv()
    layer_out[...] = (own_part + recv_part[...].astype(F32)).astype(BF16)

    r, c = grid_of(128, 64)
    low_k = jnp.where(c % 16 == r // 16, 1.0 / 16, 0.0).astype(BF16)
    low_v = jnp.where(c % 16 == r // 16 + 8, 1.0 / 16, 0.0).astype(BF16)
    for copy in home:
        copy.wait_recv()
    for sub, base, cols in ((0, acc, mine), (1, acc_in, theirs)):
        total = base[0:128, :] + dot(mix, zin[sub])
        grad_k[:, cols] = (total[:, 0:HALF] + dot(low_k, zin4[sub])).astype(BF16)
        grad_v[:, cols] = (total[:, HALF:1024] + dot(low_v, zin4[sub])).astype(BF16)
    for copy in started:
        copy.wait_send()


COPIES = 9 + 2 + 2 * (20 + 14)


def store(*refs):
    sems = refs[8]
    copies = [pltpu.make_async_copy(refs[i], refs[4 + i], sems.at[i]) for i in range(4)]
    for copy in copies:
        copy.start()
    for copy in copies:
        copy.wait()


def local(queries, key_vectors, value_vectors, slopes, w_out, grad_out):
    block = jax.ShapeDtypeStruct((B, 1024), BF16)
    vmem = pl.BlockSpec(memory_space=pltpu.VMEM)
    anywhere = pl.BlockSpec(memory_space=pl.ANY)
    results = pl.pallas_call(
        kernel,
        out_shape=[pltpu.VMEM((B, 1024), BF16)] * 4,
        in_specs=[pl.BlockSpec(memory_space=pltpu.HBM)] * 6,
        out_specs=[vmem] * 4,
        scratch_shapes=[
            pltpu.SMEM((8,), F32),
            pltpu.VMEM((KEYS, 1024), BF16),
            pltpu.VMEM((128, 1024), BF16),
            pltpu.VMEM((256, HALF), BF16),
            pltpu.VMEM((256, HALF), BF16),
            pltpu.VMEM((128, 1024), BF16),
            pltpu.VMEM((128, 1024), BF16),
            pltpu.VMEM((1024, 2048), BF16),
            pltpu.VMEM((2, 64, 1024), BF16),
            pltpu.VMEM((2, 32, 1024), BF16),
            pltpu.VMEM((2, 16, 1024), BF16),
            pltpu.VMEM((2, 16, HALF), BF16),
            pltpu.VMEM((128, HALF), BF16),
            pltpu.VMEM((128, 1024), BF16),
            pltpu.VMEM((64, 1024), BF16),
            pltpu.VMEM((32, 1024), BF16),
            pltpu.VMEM((HEADS, KEYS, 256), F32),
            pltpu.VMEM((HEADS, KEYS, 256), F32),
            pltpu.VMEM((HEADS, KEYS, 256), BF16),
            pltpu.VMEM((HEADS, KEYS, 256), BF16),
            pltpu.VMEM((768, 1024), BF16),
            pltpu.VMEM((128, 1024), F32),
            pltpu.VMEM((2, 192, 1024), BF16),
            pltpu.VMEM((8, 16, HALF), BF16),
            pltpu.VMEM((2, 192, 1024), BF16),
            pltpu.VMEM((2, 64, HALF), BF16),
            pltpu.VMEM((256, 1024), F32),
            pltpu.VMEM((128, 1024), F32),
            pltpu.VMEM((128, HALF), BF16),
            pltpu.VMEM((128, 1024), BF16),
            pltpu.VMEM((128, 1024), BF16),
            pltpu.VMEM((128, 1024), BF16),
            pltpu.VMEM((128, 1024), BF16),
            pltpu.VMEM((128, HALF), BF16),
            pltpu.SemaphoreType.DMA((COPIES,)),
            pltpu.SemaphoreType.DMA((COPIES,)),
            pltpu.SemaphoreType.DMA((8,)),
        ],
        compiler_params=pltpu.CompilerParams(
            collective_id=0, has_side_effects=True, vmem_limit_bytes=48 * 1024 * 1024
        ),
        cost_estimate=pl.CostEstimate(flops=2_700_000_000, bytes_accessed=8_000_000, transcendentals=1_000_000),
    )(*(pltpu.with_memory_space_constraint(x, pltpu.HBM) for x in (slopes, queries, key_vectors, value_vectors, grad_out, w_out)))
    return pl.pallas_call(
        store,
        out_shape=[block] * 4,
        in_specs=[vmem] * 4,
        out_specs=[pl.BlockSpec(memory_space=pltpu.HBM)] * 4,
        scratch_shapes=[pltpu.SemaphoreType.DMA((4,))],
    )(*(pltpu.with_memory_space_constraint(x, pltpu.VMEM) for x in results))


def solution(mesh):
    cut = P("ctx", "head")
    return jax.shard_map(
        local,
        mesh=mesh,
        in_specs=(cut, cut, cut, P("head"), P("head", None), cut),
        out_specs=(cut, cut, cut, cut),
        check_vma=False,
    )
```

```python
import functools
import math

import jax
import jax.numpy as jnp
from jax import lax
from jax.experimental import pallas as pl
from jax.experimental.pallas import tpu as pltpu
from jax.sharding import PartitionSpec as P

B = 128
HEAD = 128
HEADS = 2
QUARTER = 256
LANES = 512
LOG_TWO = math.log(2.0)
LOG2E = 1.0 / LOG_TWO
ROOT = 1.0 / math.sqrt(HEAD)
F32 = jnp.float32
BF16 = jnp.bfloat16
MESH = pl.DeviceIdType.MESH

L1, L2, L3, L4, L5, L6, ROWS = 512, 768, 896, 1024, 1152, 1280, 1408
S1, S2, S3, S4, S5, S6, KEYS = 256, 384, 512, 640, 768, 896, 1024


def flip(index, bits):
    out = index
    for bit in bits:
        side = (index // (1 << bit)) % 2
        out = out + (1 - 2 * side) * (1 << bit)
    return out


def bits_of(mask, first):
    return [first + i for i in range(3) if mask >> i & 1]


def dot(a, b, dims=((1,), (0,))):
    return lax.dot_general(a, b, (dims, ((), ())), preferred_element_type=F32)


def grid_of(rows, columns):
    r = lax.broadcasted_iota(jnp.int32, (rows, columns), 0)
    c = lax.broadcasted_iota(jnp.int32, (rows, columns), 1)
    return r, c


def pools(rows, ratios):
    blocks = []
    for ratio in ratios:
        r, c = grid_of(rows // ratio, rows)
        blocks.append(jnp.where(c // ratio == r, 1.0 / ratio, 0.0).astype(BF16))
    return jnp.concatenate(blocks, axis=0)


def spread(rows, parts):
    blocks = []
    for ratio, width, copies in parts:
        r, c = grid_of(rows, width * copies)
        blocks.append(jnp.where(r // ratio == c % width, 1.0 / ratio, 0.0).astype(BF16))
    return jnp.concatenate(blocks, axis=1)


def pack(x):
    return jnp.concatenate([x[:, 0:QUARTER], x[:, QUARTER:LANES]], axis=0).astype(BF16)


def in_eights(x):
    return x.reshape(x.shape[0] // 8, 8, x.shape[1])


def kernel(
    slopes_in, q, k, v, g, w_in,
    layer_out, grad_q, grad_k, grad_v,
    slopes, kv, kt, qc, gc, gown, gfar, w, s2, s3, s4, packed, a4, a5, a6,
    scores, gradw, prob, dsc, out, out3, back, n4, zin, zin4, acc, acc_core, acc_out, acc_mate,
    attn, whole, ga, send_part, recv_part, dq,
    send_sem, recv_sem, local_sem,
):
    ctx = lax.axis_index("ctx")
    head = lax.axis_index("head")
    core = ctx % 2
    place = (ctx // 2) % 2

    def cols(j):
        a, c = j // 2, j % 2
        number = (place + a - 2 * place * a) * 2 + (core + c - 2 * core * c)
        return pl.ds(pl.multiple_of(number * QUARTER, QUARTER), QUARTER)

    my_cols = pl.ds(pl.multiple_of(head * 1024, 1024), 1024)
    far_cols = pl.ds(pl.multiple_of((1 - head) * 1024, 1024), 1024)

    across = (ctx, 1 - head)
    z_peer = [[(flip(ctx, [0] * sub + bits_of(m, 1)), head) for sub in range(2)] for m in range(8)]
    other = z_peer[0][1]
    xy_peer = [None] + [(flip(ctx, bits_of(m, 4)), head) for m in range(1, 8)]

    def load(src, dst, slot):
        copy = pltpu.make_async_copy(src, dst, local_sem.at[slot])
        copy.start()
        return copy

    load_kv = []
    for j in range(4):
        into = kv.at[0:128, :] if j == 0 else kt.at[128 * (j - 1):128 * j, :]
        load_kv.append(load(k.at[:, cols(j)], into.at[:, 0:QUARTER], 2 * j))
        load_kv.append(load(v.at[:, cols(j)], into.at[:, QUARTER:LANES], 2 * j + 1))

    barrier = pltpu.get_barrier_semaphore()
    peers = [other, across] + sum(z_peer[1:], []) + xy_peer[1:]
    for peer in peers:
        pl.semaphore_signal(barrier, inc=1, device_id=peer, device_id_type=MESH)

    load_rest = [
        load(q.at[:, cols(0)], qc.at[0:128, :], 8),
        load(g, gown, 9),
        load(slopes_in, slopes, 10),
    ]
    for copy in load_kv:
        copy.wait()
    means = pools(128, (4, 8, 16))
    for j in range(4):
        pooled = dot(means, kv[0:128, :] if j == 0 else kt[128 * (j - 1):128 * j, :])
        s2[j] = pooled[0:32].astype(BF16)
        s3[j] = pooled[32:48].astype(BF16)
        s4[j] = pack(pooled[48:56])
    packed[0:16, :] = s4[0]
    load_rest.append(load(w_in, w, 11))

    pl.semaphore_wait(barrier, len(peers))

    count = [0]
    started = []

    def send(src, dst, peer):
        slot = count[0]
        count[0] += 1
        copy = pltpu.make_async_remote_copy(
            src_ref=src, dst_ref=dst, send_sem=send_sem.at[slot], recv_sem=recv_sem.at[slot],
            device_id=peer, device_id_type=MESH,
        )
        copy.start()
        started.append(copy)
        return copy

    def packed_at(m, sub):
        return packed.at[32 * m + 16 * sub:32 * m + 16 * sub + 16, :]

    in4 = [send(s4.at[1], packed_at(0, 1), other)]
    in4 += [
        send(s4.at[2 * (m % 2) + sub], packed_at(m, sub), z_peer[m][sub])
        for m in range(1, 4) for sub in range(2)
    ]

    def z_sends(source, low, rows, masks):
        return [
            send(
                source.at[2 * (m % 2) + sub],
                kv.at[low + (2 * i + sub) * rows:low + (2 * i + sub + 1) * rows, :],
                z_peer[m][sub],
            )
            for i, m in enumerate(masks)
            for sub in range(2)
        ]

    pair_peer = [None, other, z_peer[1][0], z_peer[1][1]]

    def at_pair(ref, j):
        return ref.at[128 * j:128 * j + 128, :]

    in3 = z_sends(s3, L3, 16, (4, 5, 6, 7))
    in_g = send(g, gfar, across)
    in_kv = [send(kt.at[0:128, :], at_pair(kv, 1), other)]
    in_q = [send(q.at[:, cols(j)], at_pair(qc, j), pair_peer[j]) for j in range(1, 4)]
    in2 = z_sends(s2, L2, 32, (2, 3))

    def xy_sends(half):
        copies = [send(a4.at[64 * half:64 * half + 64, :], kv.at[L4 + 64 * half:L4 + 64 * half + 64, :], xy_peer[1])]
        for m in range(2, 4):
            low = L5 + 64 * (m - 2) + 32 * half
            copies.append(send(a5.at[32 * half:32 * half + 32, :], kv.at[low:low + 32, :], xy_peer[m]))
        for m in range(4, 8):
            low = L6 + 32 * (m - 4) + 16 * half
            copies.append(send(a6.at[16 * half:16 * half + 16, :], kv.at[low:low + 16, :], xy_peer[m]))
        return copies

    for copy in in4:
        copy.wait_recv()
    r, c = grid_of(64, 128)
    at_k = (r // 8) * 16 + r % 8
    halves = pools(64, (2, 4))
    a4[0:64, 0:QUARTER] = dot(jnp.where(c == at_k, 1.0, 0.0).astype(BF16), packed[...]).astype(BF16)
    a4[0:64, QUARTER:LANES] = dot(jnp.where(c == at_k + 8, 1.0, 0.0).astype(BF16), packed[...]).astype(BF16)
    upper = dot(halves, a4[0:64, :]).astype(BF16)
    a5[0:32, :] = upper[0:32]
    a6[0:16, :] = upper[32:48]
    far = xy_sends(0)

    for copy in in3:
        copy.wait_recv()
    upper = dot(pools(128, (2, 4, 8)), kv[L3:L4, :]).astype(BF16)
    a4[64:128, :] = upper[0:64]
    a5[32:64, :] = upper[64:96]
    a6[16:32, :] = upper[96:112]
    far += xy_sends(1)

    for copy in load_rest:
        copy.wait()
    in_g.wait_recv()
    ga[...] = (
        dot(gown[...], w[:, my_cols], ((1,), (1,))) + dot(gfar[...], w[:, far_cols], ((1,), (1,)))
    ).astype(BF16)
    gc[0:128, :] = ga[:, cols(0)]
    in_ga = [send(ga.at[:, cols(j)], at_pair(gc, j), pair_peer[j]) for j in range(1, 4)]
    in_kv += [send(kt.at[128 * (j - 1):128 * j, :], at_pair(kv, j), pair_peer[j]) for j in range(2, 4)]

    lane = lax.broadcasted_iota(jnp.int32, (1, 256), 1)

    def level_bias(h, level):
        slope = slopes[(place * 2 + core) * HEADS + h]
        return (level * LOG_TWO - slope * (level + 1.0)) * LOG2E

    def bias_of(h, at):
        if at < S1:
            return jnp.where((lane < 128) == (at == 0), 0.0, level_bias(h, 0))
        return level_bias(h, {S1: 1, S2: 2, S3: 3, S4: 4, S5: 5, S6: 6}[at])

    def key_row(chip, at):
        if at < S1:
            return 256 * chip + at
        if at < S2:
            return L1 + 128 * (1 - chip) + at - S1
        return L2 + at - S2

    def key_lanes(h):
        return slice(h * HEAD, (h + 1) * HEAD)

    def value_lanes(h):
        return slice(QUARTER + h * HEAD, QUARTER + (h + 1) * HEAD)

    def queries_of(chip):
        return slice(256 * chip, 256 * chip + 256)

    def score_rows(h, chip, at):
        row = key_row(chip, at)
        rows, own = slice(row, row + 128), queries_of(chip)
        s = dot(kv[rows, key_lanes(h)], qc[own, key_lanes(h)], ((1,), (1,))) * (ROOT * LOG2E) + bias_of(h, at)
        scores[h, at:at + 128, own] = s
        gradw[h, at:at + 128, own] = dot(kv[rows, value_lanes(h)], gc[own, key_lanes(h)], ((1,), (1,)))
        return jnp.max(in_eights(s), axis=0)

    units = [(h, chip) for chip in range(2) for h in range(HEADS)]
    stats = {unit: [] for unit in units}
    group_of = {unit: {} for unit in units}

    def group(unit, places):
        h, chip = unit
        own = queries_of(chip)
        top = functools.reduce(jnp.maximum, [score_rows(h, chip, at) for at in places])
        top = jnp.max(top, axis=0, keepdims=True)
        total = jnp.zeros((8, 256), F32)
        center = jnp.zeros((8, 256), F32)
        for at in places:
            e = jnp.exp2(scores[h, at:at + 128, own] - top)
            scores[h, at:at + 128, own] = e
            total = total + jnp.sum(in_eights(e), axis=0)
            center = center + jnp.sum(in_eights(e * gradw[h, at:at + 128, own]), axis=0)
            group_of[unit][at] = len(stats[unit])
        stats[unit].append((top, jnp.sum(total, axis=0, keepdims=True), jnp.sum(center, axis=0, keepdims=True)))

    for copy in in_kv[:1] + in_q + in2 + far + in_ga:
        copy.wait_recv()
    for unit in units[0:2]:
        group(unit, (0, 128, S2, S3, S4, S5, S6))
    for unit in units[2:4]:
        group(unit, (S2, S3, S4, S5, S6))
    for copy in in_kv[1:]:
        copy.wait_recv()
    twos = pools(256, (2,))
    for chip in range(2):
        kv[L1 + 128 * chip:L1 + 128 * chip + 128, :] = dot(twos, kv[256 * chip:256 * chip + 256, :]).astype(BF16)
    for unit in units[0:2]:
        group(unit, (S1,))
    for unit in units[2:4]:
        group(unit, (0, 128, S1))

    scales, centers = {}, {}
    for unit in units:
        tops = [stat[0] for stat in stats[unit]]
        best = functools.reduce(jnp.maximum, tops)
        factors = [jnp.exp2(top - best) for top in tops]
        inverse = 1.0 / sum(f * stat[1] for f, stat in zip(factors, stats[unit]))
        centers[unit] = sum(f * stat[2] for f, stat in zip(factors, stats[unit])) * inverse
        scales[unit] = [f * inverse for f in factors]

    def normalise(h, places):
        for chip in range(2):
            own = queries_of(chip)
            for at in places:
                weight = scores[h, at:at + 128, own] * scales[h, chip][group_of[h, chip][at]]
                prob[h, at:at + 128, own] = weight.astype(BF16)
                dsc[h, at:at + 128, own] = (weight * (gradw[h, at:at + 128, own] - centers[h, chip])).astype(BF16)

    def gradients(h, low, high):
        d_key = dot(dsc[h, low:high, :], qc[:, key_lanes(h)]) * ROOT
        d_value = dot(prob[h, low:high, :], gc[:, key_lanes(h)])
        return d_key, d_value

    def put(h, low, high):
        d_key, d_value = gradients(h, low, high)
        out[low - S2:high - S2, key_lanes(h)] = d_key.astype(BF16)
        out[low - S2:high - S2, value_lanes(h)] = d_value.astype(BF16)

    def piece(low, rows):
        return out.at[low - S2:low - S2 + rows, :]

    for h in range(HEADS):
        normalise(h, (S4, S5, S6))
        put(h, S4, KEYS)

    def xy_back(half):
        copies = [send(piece(S4 + 64 * half, 64), back.at[half, 0:64, :], xy_peer[1])]
        for m in range(2, 4):
            at = 64 + 32 * (m - 2)
            copies.append(send(piece(S5 + 64 * (m - 2) + 32 * half, 32), back.at[half, at:at + 32, :], xy_peer[m]))
        for m in range(4, 8):
            at = 128 + 16 * (m - 4)
            copies.append(send(piece(S6 + 32 * (m - 4) + 16 * half, 16), back.at[half, at:at + 16, :], xy_peer[m]))
        return copies

    back_far = xy_back(1)
    back_near = xy_back(0)

    for h in range(HEADS):
        normalise(h, (S2,))
        put(h, S2, S3)
    home = [
        send(piece(S2 + (2 * i + sub) * 32, 32), zin.at[2 * (m % 2) + sub, 0:32, :], z_peer[m][sub])
        for i, m in enumerate((2, 3))
        for sub in range(2)
    ]

    for h in range(HEADS):
        normalise(h, (0, 128, S1, S3))
        d_key, d_value = gradients(h, S3, S4)
        out3[:, key_lanes(h)] = d_key
        out3[:, value_lanes(h)] = d_value

    def to_queries(h, lanes, weights):
        both = []
        for chip in range(2):
            own = queries_of(chip)
            level1 = key_row(chip, S1)
            total = (
                dot(kv[L2:ROWS, lanes], weights[h, S2:KEYS, own], ((0,), (0,)))
                + dot(kv[256 * chip:256 * chip + 256, lanes], weights[h, 0:S1, own], ((0,), (0,)))
                + dot(kv[level1:level1 + 128, lanes], weights[h, S1:S2, own], ((0,), (0,)))
            )
            both.append(total.T)
        return both

    for h in range(HEADS):
        for chip, part in enumerate(to_queries(h, value_lanes(h), prob)):
            attn[queries_of(chip), key_lanes(h)] = part.astype(BF16)
    whole[:, cols(0)] = attn[0:128, :]
    return_attn = [send(at_pair(attn, j), whole.at[:, cols(0)], pair_peer[j]) for j in (2, 3, 1)]

    for copy in back_far:
        copy.wait_recv()
    mix = spread(128, ((2, 64, 1), (4, 32, 2), (8, 16, 4)))
    out[S3 - S2:S4 - S2, :] = (out3[...] + dot(mix, back[1])).astype(BF16)
    home += [
        send(
            piece(S3 + (2 * i + sub) * 16, 16),
            zin.at[2 * (m % 2) + sub, 32 + 16 * (i // 2):48 + 16 * (i // 2), :],
            z_peer[m][sub],
        )
        for i, m in enumerate((4, 5, 6, 7))
        for sub in range(2)
    ]

    double = spread(256, ((2, 128, 1),))
    for h in range(HEADS):
        for chip in range(2):
            own, theirs = queries_of(chip), queries_of(1 - chip)
            for weights, by, lanes, factor in ((dsc, qc, key_lanes(h), ROOT), (prob, gc, value_lanes(h), 1.0)):
                level1 = dot(double, weights[h, S1:S2, theirs]).astype(BF16)
                total = dot(weights[h, 0:S1, own], by[own, key_lanes(h)]) + dot(level1, by[theirs, key_lanes(h)])
                acc[own, lanes] = total * factor
    acc_out[...] = acc[256:512, :].astype(BF16)
    home += [send(acc.at[128:256, :], acc_core, other)]
    home += [send(acc_out.at[128 * i:128 * i + 128, :], acc_mate.at[128 * i:128 * i + 128, :], pair_peer[2 + i]) for i in range(2)]

    for copy in back_near:
        copy.wait_recv()
    g4 = dot(spread(64, ((1, 64, 1), (2, 32, 2), (4, 16, 4))), back[0])
    for m in range(4):
        for sub in range(2):
            at = 16 * m + 8 * sub
            n4[2 * m + sub] = pack(g4[at:at + 8])
    zin4[0, 0:16, :] = n4[0]
    home += [send(n4.at[1], zin4.at[1, 0:16, :], other)]
    home += [
        send(n4.at[2 * m + sub], zin4.at[2 * (m % 2) + sub, 16 * (m // 2):16 * (m // 2) + 16, :], z_peer[m][sub])
        for m in range(1, 4)
        for sub in range(2)
    ]

    for h in range(HEADS):
        for chip, part in enumerate(to_queries(h, key_lanes(h), dsc)):
            dq[queries_of(chip), key_lanes(h)] = (part * ROOT).astype(BF16)
    grad_q[:, cols(0)] = dq[0:128, :]
    home += [send(at_pair(dq, j), grad_q.at[:, cols(0)], pair_peer[j]) for j in (2, 3, 1)]

    for copy in return_attn:
        copy.wait_recv()
    send_part[...] = dot(whole[...], w[:, far_cols]).astype(BF16)
    part = send(send_part, recv_part, across)
    own_part = dot(whole[...], w[:, my_cols])
    part.wait_recv()
    layer_out[...] = (own_part + recv_part[...].astype(F32)).astype(BF16)

    mix = spread(128, ((4, 32, 1), (8, 16, 2)))
    r, c = grid_of(128, 32)
    low_k = jnp.where(c % 16 == r // 16, 1.0 / 16, 0.0).astype(BF16)
    low_v = jnp.where(c % 16 == r // 16 + 8, 1.0 / 16, 0.0).astype(BF16)
    for copy in home:
        copy.wait_recv()
    bases = (acc[0:128, :], acc_core[...], acc_mate[0:128, :].astype(F32), acc_mate[128:256, :].astype(F32))
    for j, base in enumerate(bases):
        total = base + dot(mix, zin[j])
        grad_k[:, cols(j)] = (total[:, 0:QUARTER] + dot(low_k, zin4[j])).astype(BF16)
        grad_v[:, cols(j)] = (total[:, QUARTER:LANES] + dot(low_v, zin4[j])).astype(BF16)
    for copy in started:
        copy.wait_send()


COPIES = 96


def store(*refs):
    sems = refs[8]
    copies = [pltpu.make_async_copy(refs[i], refs[4 + i], sems.at[i]) for i in range(4)]
    for copy in copies:
        copy.start()
    for copy in copies:
        copy.wait()


def local(queries, key_vectors, value_vectors, slopes, w_out, grad_out):
    block = jax.ShapeDtypeStruct((B, 1024), BF16)
    vmem = pl.BlockSpec(memory_space=pltpu.VMEM)
    hbm = pl.BlockSpec(memory_space=pltpu.HBM)
    arguments = (slopes, queries, key_vectors, value_vectors, grad_out, w_out)
    results = pl.pallas_call(
        kernel,
        out_shape=[pltpu.VMEM((B, 1024), BF16)] * 4,
        in_specs=[hbm] * 6,
        out_specs=[vmem] * 4,
        scratch_shapes=[
            pltpu.SMEM((8,), F32),
            pltpu.VMEM((ROWS, LANES), BF16),
            pltpu.VMEM((384, LANES), BF16),
            pltpu.VMEM((512, QUARTER), BF16),
            pltpu.VMEM((512, QUARTER), BF16),
            pltpu.VMEM((128, 1024), BF16),
            pltpu.VMEM((128, 1024), BF16),
            pltpu.VMEM((1024, 2048), BF16),
            pltpu.VMEM((4, 32, LANES), BF16),
            pltpu.VMEM((4, 16, LANES), BF16),
            pltpu.VMEM((4, 16, QUARTER), BF16),
            pltpu.VMEM((128, QUARTER), BF16),
            pltpu.VMEM((128, LANES), BF16),
            pltpu.VMEM((64, LANES), BF16),
            pltpu.VMEM((32, LANES), BF16),
            pltpu.VMEM((HEADS, KEYS, 512), F32),
            pltpu.VMEM((HEADS, KEYS, 512), F32),
            pltpu.VMEM((HEADS, KEYS, 512), BF16),
            pltpu.VMEM((HEADS, KEYS, 512), BF16),
            pltpu.VMEM((640, LANES), BF16),
            pltpu.VMEM((128, LANES), F32),
            pltpu.VMEM((2, 192, LANES), BF16),
            pltpu.VMEM((8, 16, QUARTER), BF16),
            pltpu.VMEM((4, 64, LANES), BF16),
            pltpu.VMEM((4, 32, QUARTER), BF16),
            pltpu.VMEM((512, LANES), F32),
            pltpu.VMEM((128, LANES), F32),
            pltpu.VMEM((256, LANES), BF16),
            pltpu.VMEM((256, LANES), BF16),
            pltpu.VMEM((512, QUARTER), BF16),
            pltpu.VMEM((128, 1024), BF16),
            pltpu.VMEM((128, 1024), BF16),
            pltpu.VMEM((128, 1024), BF16),
            pltpu.VMEM((128, 1024), BF16),
            pltpu.VMEM((512, QUARTER), BF16),
            pltpu.SemaphoreType.DMA((COPIES,)),
            pltpu.SemaphoreType.DMA((COPIES,)),
            pltpu.SemaphoreType.DMA((12,)),
        ],
        compiler_params=pltpu.CompilerParams(
            collective_id=0, has_side_effects=True, vmem_limit_bytes=48 * 1024 * 1024
        ),
        cost_estimate=pl.CostEstimate(flops=2_700_000_000, bytes_accessed=8_000_000, transcendentals=1_000_000),
    )(*(pltpu.with_memory_space_constraint(x, pltpu.HBM) for x in arguments))
    return pl.pallas_call(
        store,
        out_shape=[block] * 4,
        in_specs=[vmem] * 4,
        out_specs=[hbm] * 4,
        scratch_shapes=[pltpu.SemaphoreType.DMA((4,))],
    )(*(pltpu.with_memory_space_constraint(x, pltpu.VMEM) for x in results))


def solution(mesh):
    cut = P("ctx", "head")
    return jax.shard_map(
        local,
        mesh=mesh,
        in_specs=(cut, cut, cut, P("head"), P("head", None), cut),
        out_specs=(cut, cut, cut, cut),
        check_vma=False,
    )
```

```python
import functools
import math

import jax
import jax.numpy as jnp
from jax import lax
from jax.experimental import pallas as pl
from jax.experimental.pallas import tpu as pltpu
from jax.sharding import PartitionSpec as P

B = 128
HEAD = 128
HEADS = 2
QUARTER = 256
LANES = 512
LOG_TWO = math.log(2.0)
LOG2E = 1.0 / LOG_TWO
ROOT = 1.0 / math.sqrt(HEAD)
F32 = jnp.float32
BF16 = jnp.bfloat16
MESH = pl.DeviceIdType.MESH

L1, OWN1, L2, L3, L4, L5, L6, ROWS = 0, 128, 256, 384, 512, 640, 768, 896
S1, S2, S3, S4, S5, S6, KEYS = 0, 128, 256, 384, 512, 640, 768


def flip(index, bits):
    out = index
    for bit in bits:
        side = (index // (1 << bit)) % 2
        out = out + (1 - 2 * side) * (1 << bit)
    return out


def bits_of(mask, first):
    return [first + i for i in range(3) if mask >> i & 1]


def dot(a, b, dims=((1,), (0,))):
    return lax.dot_general(a, b, (dims, ((), ())), preferred_element_type=F32)


def grid_of(rows, columns):
    r = lax.broadcasted_iota(jnp.int32, (rows, columns), 0)
    c = lax.broadcasted_iota(jnp.int32, (rows, columns), 1)
    return r, c


def pools(rows, ratios):
    blocks = []
    for ratio in ratios:
        r, c = grid_of(rows // ratio, rows)
        blocks.append(jnp.where(c // ratio == r, 1.0 / ratio, 0.0).astype(BF16))
    return jnp.concatenate(blocks, axis=0)


def spread(rows, parts):
    blocks = []
    for ratio, width, copies in parts:
        r, c = grid_of(rows, width * copies)
        blocks.append(jnp.where(r // ratio == c % width, 1.0 / ratio, 0.0).astype(BF16))
    return jnp.concatenate(blocks, axis=1)


def in_eights(x):
    return x.reshape(x.shape[0] // 8, 8, x.shape[1])


def kernel(
    slopes_in, q, k, v, g, w_in,
    layer_out, grad_q, grad_k, grad_v,
    slopes, kv, kvo, kt, qc, qm, gc, gm, gown, gfar, w, s1, s2, s3, a4, a5, a6,
    scores, gradw, prob, dsc, scores_o, gradw_o, prob_o, dsc_o, stat_out, stat_in, final_out, final_in,
    out, out123, back, zin, acc, acc_core,
    far_q, far_attn, near_q, near_attn, rest_q, rest_attn, whole, ga, send_part, recv_part,
    send_sem, recv_sem, local_sem,
):
    ctx = lax.axis_index("ctx")
    head = lax.axis_index("head")
    core = ctx % 2
    place = (ctx // 2) % 2

    def cols(j):
        a, c = j // 2, j % 2
        number = (place + a - 2 * place * a) * 2 + (core + c - 2 * core * c)
        return pl.ds(pl.multiple_of(number * QUARTER, QUARTER), QUARTER)

    my_cols = pl.ds(pl.multiple_of(head * 1024, 1024), 1024)
    far_cols = pl.ds(pl.multiple_of((1 - head) * 1024, 1024), 1024)

    across = (ctx, 1 - head)
    z_peer = [[(flip(ctx, [0] * sub + bits_of(m, 1)), head) for sub in range(2)] for m in range(8)]
    other = z_peer[0][1]
    xy_peer = [None] + [(flip(ctx, bits_of(m, 4)), head) for m in range(1, 8)]

    def load(src, dst, slot):
        copy = pltpu.make_async_copy(src, dst, local_sem.at[slot])
        copy.start()
        return copy

    load_kv = []
    for j in range(4):
        into, at = (kvo, 0) if j % 2 == 0 else (kt, 0)
        left = LANES * (j // 2)
        load_kv.append(load(k.at[:, cols(j)], into.at[0:128, left:left + QUARTER], 2 * j))
        load_kv.append(load(v.at[:, cols(j)], into.at[0:128, left + QUARTER:left + LANES], 2 * j + 1))

    barrier = pltpu.get_barrier_semaphore()
    peers = [other, across] + sum(z_peer[1:], []) + xy_peer[1:]
    for peer in peers:
        pl.semaphore_signal(barrier, inc=1, device_id=peer, device_id_type=MESH)

    load_rest = [
        load(q.at[:, cols(0)], qc.at[0:128, :], 8),
        load(q.at[:, cols(2)], qm.at[0:128, :], 9),
        load(g, gown, 10),
        load(slopes_in, slopes, 11),
    ]
    stat_out[...] = jnp.zeros_like(stat_out)
    final_out[...] = jnp.zeros_like(final_out)
    for copy in load_kv:
        copy.wait()
    load_rest.append(load(w_in, w, 12))
    means = pools(128, (2, 4, 8))
    for j in range(4):
        left = LANES * (j // 2)
        pooled = dot(means, kvo[0:128, left:left + LANES] if j % 2 == 0 else kt[:, left:left + LANES]).astype(BF16)
        s1[j] = pooled[0:64]
        s2[j] = pooled[64:96]
        s3[j] = pooled[96:112]

    pl.semaphore_wait(barrier, len(peers))

    count = [0]
    started = []

    def send(src, dst, peer):
        slot = count[0]
        count[0] += 1
        copy = pltpu.make_async_remote_copy(
            src_ref=src, dst_ref=dst, send_sem=send_sem.at[slot], recv_sem=recv_sem.at[slot],
            device_id=peer, device_id_type=MESH,
        )
        copy.start()
        started.append(copy)
        return copy

    pair_peer = [None, other, z_peer[1][0], z_peer[1][1]]

    def at_pair(ref, j):
        return ref.at[128 * j:128 * j + 128, :]

    def z_sends(source, low, rows, masks):
        return [
            send(
                source.at[2 * (m % 2) + sub],
                kv.at[low + (2 * i + sub) * rows:low + (2 * i + sub + 1) * rows, :],
                z_peer[m][sub],
            )
            for i, m in enumerate(masks)
            for sub in range(2)
        ]

    in3 = z_sends(s3, L3, 16, (4, 5, 6, 7))
    in_g = send(g, gfar, across)
    in_kv = send(kt, kvo.at[128:256, :], other)
    in_q_core = [send(q.at[:, cols(1)], at_pair(qc, 1), other), send(q.at[:, cols(3)], at_pair(qm, 1), other)]
    in2 = z_sends(s2, L2, 32, (2, 3))
    in1 = z_sends(s1, L1, 64, (1,))
    in_q = [send(q.at[:, cols(j)], at_pair(qc, j), pair_peer[j]) for j in range(2, 4)]

    in_kv.wait_recv()
    kv[OWN1:L2, :] = dot(pools(256, (2,)), kvo[:, 0:LANES]).astype(BF16)
    a4[0:16, :] = dot(pools(256, (16,)), kvo[:, 0:LANES]).astype(BF16)

    def xy_sends(half):
        copies = [send(a4.at[64 * half:64 * half + 64, :], kv.at[L4 + 64 * half:L4 + 64 * half + 64, :], xy_peer[1])]
        for m in range(2, 4):
            low = L5 + 64 * (m - 2) + 32 * half
            copies.append(send(a5.at[32 * half:32 * half + 32, :], kv.at[low:low + 32, :], xy_peer[m]))
        for m in range(4, 8):
            low = L6 + 32 * (m - 4) + 16 * half
            copies.append(send(a6.at[16 * half:16 * half + 16, :], kv.at[low:low + 16, :], xy_peer[m]))
        return copies

    for copy in in3:
        copy.wait_recv()
    upper = dot(pools(128, (2, 4, 8)), kv[L3:L4, :]).astype(BF16)
    a4[64:128, :] = upper[0:64]
    a5[32:64, :] = upper[64:96]
    a6[16:32, :] = upper[96:112]
    far = xy_sends(1)

    for copy in load_rest:
        copy.wait()
    in_g.wait_recv()
    ga[...] = (
        dot(gown[...], w[:, my_cols], ((1,), (1,))) + dot(gfar[...], w[:, far_cols], ((1,), (1,)))
    ).astype(BF16)
    in_ga = [send(ga.at[:, cols(j)], at_pair(gc, j), pair_peer[j]) for j in range(2, 4)]
    in_ga_core = [send(ga.at[:, cols(1)], at_pair(gc, 1), other), send(ga.at[:, cols(3)], at_pair(gm, 1), other)]
    gc[0:128, :] = ga[:, cols(0)]
    gm[0:128, :] = ga[:, cols(2)]

    lane = lax.broadcasted_iota(jnp.int32, (1, 256), 1)

    def level_bias(t, h, level):
        slope = slopes[((place + t - 2 * place * t) * 2 + core) * HEADS + h]
        return (level * LOG_TWO - slope * (level + 1.0)) * LOG2E

    def key_lanes(h, t=0):
        return slice(LANES * t + h * HEAD, LANES * t + (h + 1) * HEAD)

    def value_lanes(h, t=0):
        return slice(LANES * t + QUARTER + h * HEAD, LANES * t + QUARTER + (h + 1) * HEAD)

    def queries_of(chip):
        return slice(256 * chip, 256 * chip + 256)

    def head_of(h):
        return slice(h * HEAD, (h + 1) * HEAD)

    def across_lanes(x):
        return jnp.sum(x, axis=0, keepdims=True)

    def own_stats(t, h):
        by, to = (qc, gc) if t == 0 else (qm, gm)
        u = 2 * t + h
        tops = []
        for at in (0, 128):
            rows = slice(at, at + 128)
            bias = jnp.where((lane < 128) == (at == 0), 0.0, level_bias(t, h, 0))
            s = dot(kvo[rows, key_lanes(h, t)], by[0:256, head_of(h)], ((1,), (1,))) * (ROOT * LOG2E) + bias
            scores_o[u, rows, :] = s
            tops.append(jnp.max(in_eights(s), axis=0))
        top = jnp.max(jnp.maximum(tops[0], tops[1]), axis=0, keepdims=True)
        total = jnp.zeros((8, 256), F32)
        center = jnp.zeros((8, 256), F32)
        for at in (0, 128):
            rows = slice(at, at + 128)
            e = jnp.exp2(scores_o[u, rows, :] - top)
            scores_o[u, rows, :] = e
            toward = dot(kvo[rows, value_lanes(h, t)], to[0:256, head_of(h)], ((1,), (1,)))
            gradw_o[u, rows, :] = toward
            total = total + jnp.sum(in_eights(e), axis=0)
            center = center + jnp.sum(in_eights(e * toward), axis=0)
        return top, across_lanes(total), across_lanes(center)

    for copy in in_q_core + in_ga_core:
        copy.wait_recv()
    for h in range(HEADS):
        for n, stat in enumerate(own_stats(1, h)):
            stat_out[3 * h + n:3 * h + n + 1, :] = stat
    in_stat = send(stat_out, stat_in, z_peer[1][0])
    near_stats = [own_stats(0, h) for h in range(HEADS)]

    for copy in in1 + in2:
        copy.wait_recv()
    a4[16:32, :] = dot(pools(128, (8,)), kv[L1:L1 + 128, :]).astype(BF16)
    a4[32:64, :] = dot(pools(128, (4,)), kv[L2:L3, :]).astype(BF16)
    upper = dot(pools(64, (2, 4)), a4[0:64, :]).astype(BF16)
    a5[0:32, :] = upper[0:32]
    a6[0:16, :] = upper[32:48]
    far += xy_sends(0)

    def key_row(chip, at):
        return L1 + 128 * chip if at == S1 else L2 + at - S2

    def exponents(unit, places):
        h, chip = unit
        own = queries_of(chip)
        tops = []
        for at in places:
            row = key_row(chip, at)
            s = dot(kv[row:row + 128, key_lanes(h)], qc[own, head_of(h)], ((1,), (1,))) * (ROOT * LOG2E)
            s = s + level_bias(0, h, at // 128 + 1)
            scores[h, at:at + 128, own] = s
            tops.append(jnp.max(in_eights(s), axis=0))
        top = jnp.max(functools.reduce(jnp.maximum, tops), axis=0, keepdims=True)
        total = jnp.zeros((8, 256), F32)
        for at in places:
            e = jnp.exp2(scores[h, at:at + 128, own] - top)
            scores[h, at:at + 128, own] = e
            total = total + jnp.sum(in_eights(e), axis=0)
        return top, across_lanes(total)

    def toward_center(unit, places):
        h, chip = unit
        own = queries_of(chip)
        center = jnp.zeros((8, 256), F32)
        for at in places:
            row = key_row(chip, at)
            toward = dot(kv[row:row + 128, value_lanes(h)], gc[own, head_of(h)], ((1,), (1,)))
            gradw[h, at:at + 128, own] = toward
            center = center + jnp.sum(in_eights(scores[h, at:at + 128, own] * toward), axis=0)
        return across_lanes(center)

    units = [(h, chip) for chip in range(2) for h in range(HEADS)]
    parts = ((S1, S2, S3), (S4, S5, S6))
    tops = {unit: [] for unit in units}
    totals = {unit: [] for unit in units}
    sums = {unit: [] for unit in units}

    def add_exponents(unit, places):
        top, total = exponents(unit, places)
        tops[unit].append(top)
        totals[unit].append(total)

    for unit in units[0:2]:
        add_exponents(unit, parts[0])
        sums[unit].append(toward_center(unit, parts[0]))
    for copy in in_q:
        copy.wait_recv()
    for unit in units[2:4]:
        add_exponents(unit, parts[0])
    for copy in far:
        copy.wait_recv()
    for unit in units[0:2]:
        add_exponents(unit, parts[1])
        sums[unit].append(toward_center(unit, parts[1]))
    for unit in units[2:4]:
        add_exponents(unit, parts[1])
    in_stat.wait_recv()
    for copy in in_ga:
        copy.wait_recv()
    for unit in units[2:4]:
        for places in parts:
            sums[unit].append(toward_center(unit, places))

    scales, centers = {}, {}
    for unit in units:
        h, chip = unit
        if chip == 0:
            stat = near_stats[h]
        else:
            stat = tuple(stat_in[3 * h + n:3 * h + n + 1, :] for n in range(3))
        every = tops[unit] + [stat[0]]
        best = functools.reduce(jnp.maximum, every)
        factors = [jnp.exp2(top - best) for top in every]
        inverse = 1.0 / sum(f * total for f, total in zip(factors, totals[unit] + [stat[1]]))
        centers[unit] = sum(f * part for f, part in zip(factors, sums[unit] + [stat[2]])) * inverse
        scales[unit] = [f * inverse for f in factors]
        if chip == 1:
            final_out[2 * h:2 * h + 1, :] = scales[unit][2]
            final_out[2 * h + 1:2 * h + 2, :] = centers[unit]
    in_final = send(final_out, final_in, z_peer[1][0])

    def normalise(h, n):
        for chip in range(2):
            own = queries_of(chip)
            for at in parts[n]:
                weight = scores[h, at:at + 128, own] * scales[h, chip][n]
                prob[h, at:at + 128, own] = weight.astype(BF16)
                dsc[h, at:at + 128, own] = (weight * (gradw[h, at:at + 128, own] - centers[h, chip])).astype(BF16)

    def gradients(h, low, high, own=slice(0, 512)):
        d_key = dot(dsc[h, low:high, own], qc[own, head_of(h)]) * ROOT
        d_value = dot(prob[h, low:high, own], gc[own, head_of(h)])
        return d_key, d_value

    def piece(low, rows):
        return out.at[low:low + rows, :]

    for h in range(HEADS):
        normalise(h, 1)
        d_key, d_value = gradients(h, S4, KEYS)
        out[S4:KEYS, key_lanes(h)] = d_key.astype(BF16)
        out[S4:KEYS, value_lanes(h)] = d_value.astype(BF16)

    def xy_back(half):
        copies = [send(piece(S4 + 64 * half, 64), back.at[half, 0:64, :], xy_peer[1])]
        for m in range(2, 4):
            at = 64 + 32 * (m - 2)
            copies.append(send(piece(S5 + 64 * (m - 2) + 32 * half, 32), back.at[half, at:at + 32, :], xy_peer[m]))
        for m in range(4, 8):
            at = 128 + 16 * (m - 4)
            copies.append(send(piece(S6 + 32 * (m - 4) + 16 * half, 16), back.at[half, at:at + 16, :], xy_peer[m]))
        return copies

    back_near = xy_back(0)
    back_far = xy_back(1)

    for h in range(HEADS):
        normalise(h, 0)

    def to_queries(h, chip, lanes, weights):
        own, level1 = queries_of(chip), key_row(chip, S1)
        total = dot(kv[L2:ROWS, lanes], weights[h, S2:KEYS, own], ((0,), (0,)))
        return (total + dot(kv[level1:level1 + 128, lanes], weights[h, S1:S2, own], ((0,), (0,)))).T

    for h in range(HEADS):
        far_attn[:, head_of(h)] = to_queries(h, 1, value_lanes(h), prob).astype(BF16)
    in_rest_attn = [send(at_pair(far_attn, i), rest_attn.at[i], pair_peer[2 + i]) for i in range(2)]
    for h in range(HEADS):
        far_q[:, head_of(h)] = (to_queries(h, 1, key_lanes(h), dsc) * ROOT).astype(BF16)
    in_rest_q = [send(at_pair(far_q, i), rest_q.at[i], pair_peer[2 + i]) for i in range(2)]

    for h in range(HEADS):
        d_key, d_value = gradients(h, S2, S4)
        out123[128:384, key_lanes(h)] = d_key
        out123[128:384, value_lanes(h)] = d_value
        d_key, d_value = gradients(h, S1, S2, queries_of(0))
        out123[0:128, key_lanes(h)] = d_key
        out123[0:128, value_lanes(h)] = d_value

    double = spread(256, ((2, 128, 1),))
    in_near = []
    for t in range(2):
        if t == 1:
            in_final.wait_recv()
        by, to = (qc, gc) if t == 0 else (qm, gm)
        for h in range(HEADS):
            u = 2 * t + h
            if t == 0:
                scale, center = scales[h, 0][2], centers[h, 0]
            else:
                scale, center = final_in[2 * h:2 * h + 1, :], final_in[2 * h + 1:2 * h + 2, :]
            weight = scores_o[u] * scale
            prob_o[u] = weight.astype(BF16)
            dsc_o[u] = (weight * (gradw_o[u] - center)).astype(BF16)
            for weights, source, beyond, lanes, factor in (
                (dsc_o, by, dsc, key_lanes(h, t), ROOT), (prob_o, to, prob, value_lanes(h, t), 1.0)
            ):
                total = dot(weights[u], source[0:256, head_of(h)])
                if t == 0:
                    level1 = dot(double, beyond[h, S1:S2, 256:512]).astype(BF16)
                    total = total + dot(level1, source[256:512, head_of(h)])
                acc[:, lanes] = total * factor
            attn_part = dot(kvo[:, value_lanes(h, t)], prob_o[u], ((0,), (0,))).T
            q_part = dot(kvo[:, key_lanes(h, t)], dsc_o[u], ((0,), (0,))).T
            if t == 0:
                attn_part = attn_part + to_queries(h, 0, value_lanes(h), prob)
                q_part = q_part + to_queries(h, 0, key_lanes(h), dsc)
            near_attn[t, :, head_of(h)] = attn_part.astype(BF16)
            near_q[t, :, head_of(h)] = (q_part * ROOT).astype(BF16)
        if t == 0:
            in_near += [send(near_attn.at[0, 128:256, :], whole.at[:, cols(0)], other)]
            in_near += [send(near_q.at[0, 128:256, :], grad_q.at[:, cols(0)], other)]
        else:
            in_near += [send(near_attn.at[1, 128:256, :], rest_attn.at[2], other)]
            in_near += [send(near_q.at[1, 128:256, :], rest_q.at[2], other)]

    for copy in back_near:
        copy.wait_recv()
    g4 = dot(spread(64, ((1, 64, 1), (2, 32, 2), (4, 16, 4))), back[0]).astype(BF16)
    out[0:128, :] = (out123[0:128, :] + dot(spread(128, ((8, 16, 1),)), g4[16:32])).astype(BF16)
    out[128:256, :] = (out123[128:256, :] + dot(spread(128, ((4, 32, 1),)), g4[32:64])).astype(BF16)
    home = [send(piece(S1 + 64 * sub, 64), zin.at[2 + sub, 0:64, :], z_peer[1][sub]) for sub in range(2)]
    home += [
        send(piece(S2 + (2 * i + sub) * 32, 32), zin.at[2 * (m % 2) + sub, 64:96, :], z_peer[m][sub])
        for i, m in enumerate((2, 3))
        for sub in range(2)
    ]
    acc[:, 0:LANES] += dot(spread(256, ((16, 16, 1),)), g4[0:16])
    home += [send(acc.at[128:256, :], acc_core, other)]

    for copy in back_far:
        copy.wait_recv()
    mix = spread(128, ((2, 64, 1), (4, 32, 2), (8, 16, 4)))
    out[S3:S4, :] = (out123[256:384, :] + dot(mix, back[1])).astype(BF16)
    home += [
        send(
            piece(S3 + (2 * i + sub) * 16, 16),
            zin.at[2 * (m % 2) + sub, 96 + 16 * (i // 2):112 + 16 * (i // 2), :],
            z_peer[m][sub],
        )
        for i, m in enumerate((4, 5, 6, 7))
        for sub in range(2)
    ]

    whole[:, cols(0)] = near_attn[0, 0:128, :]
    grad_q[:, cols(0)] = near_q[0, 0:128, :]
    for copy in in_near + in_rest_attn:
        copy.wait_recv()
    whole[:, cols(2)] = (near_attn[1, 0:128, :].astype(F32) + rest_attn[0].astype(F32)).astype(BF16)
    whole[:, cols(3)] = (rest_attn[2].astype(F32) + rest_attn[1].astype(F32)).astype(BF16)
    send_part[...] = dot(whole[...], w[:, far_cols]).astype(BF16)
    part = send(send_part, recv_part, across)
    for copy in in_rest_q:
        copy.wait_recv()
    grad_q[:, cols(2)] = (near_q[1, 0:128, :].astype(F32) + rest_q[0].astype(F32)).astype(BF16)
    grad_q[:, cols(3)] = (rest_q[2].astype(F32) + rest_q[1].astype(F32)).astype(BF16)
    own_part = dot(whole[...], w[:, my_cols])
    part.wait_recv()
    layer_out[...] = (own_part + recv_part[...].astype(F32)).astype(BF16)

    mix = spread(128, ((2, 64, 1), (4, 32, 1), (8, 16, 2)))
    for copy in home:
        copy.wait_recv()
    bases = (acc[0:128, 0:LANES], acc_core[:, 0:LANES], acc[0:128, LANES:1024], acc_core[:, LANES:1024])
    for j, base in enumerate(bases):
        low = 64 if j < 2 else 0
        total = (base + dot(mix[:, low:128], zin[j, low:128, :])).astype(BF16)
        grad_k[:, cols(j)] = total[:, 0:QUARTER]
        grad_v[:, cols(j)] = total[:, QUARTER:LANES]
    for copy in started:
        copy.wait_send()


COPIES = 96


def store(*refs):
    sems = refs[8]
    copies = [pltpu.make_async_copy(refs[i], refs[4 + i], sems.at[i]) for i in range(4)]
    for copy in copies:
        copy.start()
    for copy in copies:
        copy.wait()


def local(queries, key_vectors, value_vectors, slopes, w_out, grad_out):
    block = jax.ShapeDtypeStruct((B, 1024), BF16)
    vmem = pl.BlockSpec(memory_space=pltpu.VMEM)
    hbm = pl.BlockSpec(memory_space=pltpu.HBM)
    arguments = (slopes, queries, key_vectors, value_vectors, grad_out, w_out)
    results = pl.pallas_call(
        kernel,
        out_shape=[pltpu.VMEM((B, 1024), BF16)] * 4,
        in_specs=[hbm] * 6,
        out_specs=[vmem] * 4,
        scratch_shapes=[
            pltpu.SMEM((8,), F32),
            pltpu.VMEM((ROWS, LANES), BF16),
            pltpu.VMEM((256, 1024), BF16),
            pltpu.VMEM((128, 1024), BF16),
            pltpu.VMEM((512, QUARTER), BF16),
            pltpu.VMEM((256, QUARTER), BF16),
            pltpu.VMEM((512, QUARTER), BF16),
            pltpu.VMEM((256, QUARTER), BF16),
            pltpu.VMEM((128, 1024), BF16),
            pltpu.VMEM((128, 1024), BF16),
            pltpu.VMEM((1024, 2048), BF16),
            pltpu.VMEM((4, 64, LANES), BF16),
            pltpu.VMEM((4, 32, LANES), BF16),
            pltpu.VMEM((4, 16, LANES), BF16),
            pltpu.VMEM((128, LANES), BF16),
            pltpu.VMEM((64, LANES), BF16),
            pltpu.VMEM((32, LANES), BF16),
            pltpu.VMEM((HEADS, KEYS, 512), F32),
            pltpu.VMEM((HEADS, KEYS, 512), F32),
            pltpu.VMEM((HEADS, KEYS, 512), BF16),
            pltpu.VMEM((HEADS, KEYS, 512), BF16),
            pltpu.VMEM((4, 256, 256), F32),
            pltpu.VMEM((4, 256, 256), F32),
            pltpu.VMEM((4, 256, 256), BF16),
            pltpu.VMEM((4, 256, 256), BF16),
            pltpu.VMEM((8, 256), F32),
            pltpu.VMEM((8, 256), F32),
            pltpu.VMEM((8, 256), F32),
            pltpu.VMEM((8, 256), F32),
            pltpu.VMEM((KEYS, LANES), BF16),
            pltpu.VMEM((384, LANES), F32),
            pltpu.VMEM((2, 192, LANES), BF16),
            pltpu.VMEM((4, 128, LANES), BF16),
            pltpu.VMEM((256, 1024), F32),
            pltpu.VMEM((128, 1024), F32),
            pltpu.VMEM((256, QUARTER), BF16),
            pltpu.VMEM((256, QUARTER), BF16),
            pltpu.VMEM((2, 256, QUARTER), BF16),
            pltpu.VMEM((2, 256, QUARTER), BF16),
            pltpu.VMEM((3, 128, QUARTER), BF16),
            pltpu.VMEM((3, 128, QUARTER), BF16),
            pltpu.VMEM((128, 1024), BF16),
            pltpu.VMEM((128, 1024), BF16),
            pltpu.VMEM((128, 1024), BF16),
            pltpu.VMEM((128, 1024), BF16),
            pltpu.SemaphoreType.DMA((COPIES,)),
            pltpu.SemaphoreType.DMA((COPIES,)),
            pltpu.SemaphoreType.DMA((13,)),
        ],
        compiler_params=pltpu.CompilerParams(
            collective_id=0, has_side_effects=True, vmem_limit_bytes=48 * 1024 * 1024
        ),
        cost_estimate=pl.CostEstimate(flops=2_700_000_000, bytes_accessed=8_000_000, transcendentals=1_000_000),
    )(*(pltpu.with_memory_space_constraint(x, pltpu.HBM) for x in arguments))
    return pl.pallas_call(
        store,
        out_shape=[block] * 4,
        in_specs=[vmem] * 4,
        out_specs=[hbm] * 4,
        scratch_shapes=[pltpu.SemaphoreType.DMA((4,))],
    )(*(pltpu.with_memory_space_constraint(x, pltpu.VMEM) for x in results))


def solution(mesh):
    cut = P("ctx", "head")
    return jax.shard_map(
        local,
        mesh=mesh,
        in_specs=(cut, cut, cut, P("head"), P("head", None), cut),
        out_specs=(cut, cut, cut, cut),
        check_vma=False,
    )
```

```python
import functools
import math

import jax
import jax.numpy as jnp
from jax import lax
from jax.experimental import pallas as pl
from jax.experimental.pallas import tpu as pltpu
from jax.sharding import PartitionSpec as P

B = 128
HEAD = 128
HEADS = 2
QUARTER = 256
LANES = 512
LOG_TWO = math.log(2.0)
LOG2E = 1.0 / LOG_TWO
ROOT = 1.0 / math.sqrt(HEAD)
F32 = jnp.float32
BF16 = jnp.bfloat16
MESH = pl.DeviceIdType.MESH

L1, OWN1, L2, L3, L4, L5, L6, ROWS = 0, 128, 256, 384, 512, 640, 768, 896
S1, S2, S3, S4, S5, S6, KEYS = 0, 128, 256, 384, 512, 640, 768


def flip(index, bits):
    out = index
    for bit in bits:
        side = (index // (1 << bit)) % 2
        out = out + (1 - 2 * side) * (1 << bit)
    return out


def bits_of(mask, first):
    return [first + i for i in range(3) if mask >> i & 1]


def dot(a, b, dims=((1,), (0,))):
    return lax.dot_general(a, b, (dims, ((), ())), preferred_element_type=F32)


def grid_of(rows, columns):
    r = lax.broadcasted_iota(jnp.int32, (rows, columns), 0)
    c = lax.broadcasted_iota(jnp.int32, (rows, columns), 1)
    return r, c


def pools(rows, ratios):
    blocks = []
    for ratio in ratios:
        r, c = grid_of(rows // ratio, rows)
        blocks.append(jnp.where(c // ratio == r, 1.0 / ratio, 0.0).astype(BF16))
    return jnp.concatenate(blocks, axis=0)


def spread(rows, parts):
    blocks = []
    for ratio, width, copies in parts:
        r, c = grid_of(rows, width * copies)
        blocks.append(jnp.where(r // ratio == c % width, 1.0 / ratio, 0.0).astype(BF16))
    return jnp.concatenate(blocks, axis=1)


def in_eights(x):
    return x.reshape(x.shape[0] // 8, 8, x.shape[1])


def kernel(
    slopes_in, q, k, v, g, w_in,
    layer_out, grad_q, grad_k, grad_v,
    slopes, kv, kvo, kt, qc, qm, gc, gm, gown, gfar, w, s1, s2, s3, mate3, a4, a5, a6,
    scores, gradw, prob, dsc, scores_o, gradw_o, prob_o, dsc_o, stat_out, stat_in, final_out, final_in,
    out, out123, back, zin, acc, acc_core,
    far_q, far_attn, near_q, near_attn, rest_q, rest_attn, whole, ga, send_part, recv_part,
    send_sem, recv_sem, local_sem,
):
    ctx = lax.axis_index("ctx")
    head = lax.axis_index("head")
    core = ctx % 2
    place = (ctx // 2) % 2

    def cols(j):
        a, c = j // 2, j % 2
        number = (place + a - 2 * place * a) * 2 + (core + c - 2 * core * c)
        return pl.ds(pl.multiple_of(number * QUARTER, QUARTER), QUARTER)

    my_cols = pl.ds(pl.multiple_of(head * 1024, 1024), 1024)
    far_cols = pl.ds(pl.multiple_of((1 - head) * 1024, 1024), 1024)

    across = (ctx, 1 - head)
    z_peer = [[(flip(ctx, [0] * sub + bits_of(m, 1)), head) for sub in range(2)] for m in range(8)]
    other = z_peer[0][1]
    xy_peer = [None] + [(flip(ctx, bits_of(m, 4)), head) for m in range(1, 8)]

    def load(src, dst, slot):
        copy = pltpu.make_async_copy(src, dst, local_sem.at[slot])
        copy.start()
        return copy

    load_kv = []
    for j in range(4):
        into, at = (kvo, 0) if j % 2 == 0 else (kt, 0)
        left = LANES * (j // 2)
        load_kv.append(load(k.at[:, cols(j)], into.at[0:128, left:left + QUARTER], 2 * j))
        load_kv.append(load(v.at[:, cols(j)], into.at[0:128, left + QUARTER:left + LANES], 2 * j + 1))

    barrier = pltpu.get_barrier_semaphore()
    peers = [other, across] + sum(z_peer[1:], []) + xy_peer[1:]
    for peer in peers:
        pl.semaphore_signal(barrier, inc=1, device_id=peer, device_id_type=MESH)

    load_rest = [
        load(q.at[:, cols(0)], qc.at[0:128, :], 8),
        load(q.at[:, cols(2)], qm.at[0:128, :], 9),
        load(g, gown, 10),
        load(slopes_in, slopes, 11),
    ]
    stat_out[...] = jnp.zeros_like(stat_out)
    final_out[...] = jnp.zeros_like(final_out)
    for copy in load_kv:
        copy.wait()
    load_rest.append(load(w_in, w, 12))
    means = pools(128, (2, 4, 8))
    for j in range(4):
        left = LANES * (j // 2)
        pooled = dot(means, kvo[0:128, left:left + LANES] if j % 2 == 0 else kt[:, left:left + LANES]).astype(BF16)
        s1[j] = pooled[0:64]
        s2[j] = pooled[64:96]
        s3[j] = pooled[96:112]

    pl.semaphore_wait(barrier, len(peers))

    count = [0]
    started = []

    def send(src, dst, peer):
        slot = count[0]
        count[0] += 1
        copy = pltpu.make_async_remote_copy(
            src_ref=src, dst_ref=dst, send_sem=send_sem.at[slot], recv_sem=recv_sem.at[slot],
            device_id=peer, device_id_type=MESH,
        )
        copy.start()
        started.append(copy)
        return copy

    pair_peer = [None, other, z_peer[1][0], z_peer[1][1]]

    def at_pair(ref, j):
        return ref.at[128 * j:128 * j + 128, :]

    def z_sends(source, low, rows, masks):
        return [
            send(
                source.at[2 * (m % 2) + sub],
                kv.at[low + (2 * i + sub) * rows:low + (2 * i + sub + 1) * rows, :],
                z_peer[m][sub],
            )
            for i, m in enumerate(masks)
            for sub in range(2)
        ]

    in3 = z_sends(s3, L3, 16, (4, 5, 6, 7))
    in_mate = [send(s3.at[2 + sub], mate3.at[16 * sub:16 * sub + 16, :], z_peer[1][sub]) for sub in range(2)]
    in2 = z_sends(s2, L2, 32, (2, 3))
    in1 = z_sends(s1, L1, 64, (1,))
    in_kv = send(kt, kvo.at[128:256, :], other)
    in_g = send(g, gfar, across)
    in_q_core = [send(q.at[:, cols(1)], at_pair(qc, 1), other), send(q.at[:, cols(3)], at_pair(qm, 1), other)]
    in_q = [send(q.at[:, cols(j)], at_pair(qc, j), pair_peer[j]) for j in range(2, 4)]

    in_kv.wait_recv()
    kv[OWN1:L2, :] = dot(pools(256, (2,)), kvo[:, 0:LANES]).astype(BF16)
    a4[0:16, :] = dot(pools(256, (16,)), kvo[:, 0:LANES]).astype(BF16)

    def xy_sends(half):
        copies = [send(a4.at[64 * half:64 * half + 64, :], kv.at[L4 + 64 * half:L4 + 64 * half + 64, :], xy_peer[1])]
        for m in range(2, 4):
            low = L5 + 64 * (m - 2) + 32 * half
            copies.append(send(a5.at[32 * half:32 * half + 32, :], kv.at[low:low + 32, :], xy_peer[m]))
        for m in range(4, 8):
            low = L6 + 32 * (m - 4) + 16 * half
            copies.append(send(a6.at[16 * half:16 * half + 16, :], kv.at[low:low + 16, :], xy_peer[m]))
        return copies

    for copy in in3:
        copy.wait_recv()
    upper = dot(pools(128, (2, 4, 8)), kv[L3:L4, :]).astype(BF16)
    a4[64:128, :] = upper[0:64]
    a5[32:64, :] = upper[64:96]
    a6[16:32, :] = upper[96:112]
    far = xy_sends(1)

    for copy in load_rest:
        copy.wait()
    in_g.wait_recv()
    ga[...] = (
        dot(gown[...], w[:, my_cols], ((1,), (1,))) + dot(gfar[...], w[:, far_cols], ((1,), (1,)))
    ).astype(BF16)
    in_ga = [send(ga.at[:, cols(j)], at_pair(gc, j), pair_peer[j]) for j in range(2, 4)]
    in_ga_core = [send(ga.at[:, cols(1)], at_pair(gc, 1), other), send(ga.at[:, cols(3)], at_pair(gm, 1), other)]
    gc[0:128, :] = ga[:, cols(0)]
    gm[0:128, :] = ga[:, cols(2)]

    lane = lax.broadcasted_iota(jnp.int32, (1, 256), 1)

    def level_bias(t, h, level):
        slope = slopes[((place + t - 2 * place * t) * 2 + core) * HEADS + h]
        return (level * LOG_TWO - slope * (level + 1.0)) * LOG2E

    def key_lanes(h, t=0):
        return slice(LANES * t + h * HEAD, LANES * t + (h + 1) * HEAD)

    def value_lanes(h, t=0):
        return slice(LANES * t + QUARTER + h * HEAD, LANES * t + QUARTER + (h + 1) * HEAD)

    def queries_of(chip):
        return slice(256 * chip, 256 * chip + 256)

    def head_of(h):
        return slice(h * HEAD, (h + 1) * HEAD)

    def across_lanes(x):
        return jnp.sum(x, axis=0, keepdims=True)

    def own_stats(t, h):
        by, to = (qc, gc) if t == 0 else (qm, gm)
        u = 2 * t + h
        tops = []
        for at in (0, 128):
            rows = slice(at, at + 128)
            bias = jnp.where((lane < 128) == (at == 0), 0.0, level_bias(t, h, 0))
            s = dot(kvo[rows, key_lanes(h, t)], by[0:256, head_of(h)], ((1,), (1,))) * (ROOT * LOG2E) + bias
            scores_o[u, rows, :] = s
            tops.append(jnp.max(in_eights(s), axis=0))
        top = jnp.max(jnp.maximum(tops[0], tops[1]), axis=0, keepdims=True)
        total = jnp.zeros((8, 256), F32)
        center = jnp.zeros((8, 256), F32)
        for at in (0, 128):
            rows = slice(at, at + 128)
            e = jnp.exp2(scores_o[u, rows, :] - top)
            scores_o[u, rows, :] = e
            toward = dot(kvo[rows, value_lanes(h, t)], to[0:256, head_of(h)], ((1,), (1,)))
            gradw_o[u, rows, :] = toward
            total = total + jnp.sum(in_eights(e), axis=0)
            center = center + jnp.sum(in_eights(e * toward), axis=0)
        return top, across_lanes(total), across_lanes(center)

    for copy in in_mate + in2:
        copy.wait_recv()
    a4[16:32, :] = dot(pools(32, (2,)), mate3[...]).astype(BF16)
    a4[32:64, :] = dot(pools(128, (4,)), kv[L2:L3, :]).astype(BF16)
    upper = dot(pools(64, (2, 4)), a4[0:64, :]).astype(BF16)
    a5[0:32, :] = upper[0:32]
    a6[0:16, :] = upper[32:48]
    far += xy_sends(0)

    for copy in in_q_core + in_ga_core:
        copy.wait_recv()
    near_stats = [own_stats(0, h) for h in range(HEADS)]

    for h in range(HEADS):
        for n, stat in enumerate(own_stats(1, h)):
            stat_out[3 * h + n:3 * h + n + 1, :] = stat
    in_stat = send(stat_out, stat_in, z_peer[1][0])

    def key_row(chip, at):
        return L1 + 128 * chip if at == S1 else L2 + at - S2

    def exponents(unit, places):
        h, chip = unit
        own = queries_of(chip)
        tops = []
        for at in places:
            row = key_row(chip, at)
            s = dot(kv[row:row + 128, key_lanes(h)], qc[own, head_of(h)], ((1,), (1,))) * (ROOT * LOG2E)
            s = s + level_bias(0, h, at // 128 + 1)
            scores[h, at:at + 128, own] = s
            tops.append(jnp.max(in_eights(s), axis=0))
        top = jnp.max(functools.reduce(jnp.maximum, tops), axis=0, keepdims=True)
        total = jnp.zeros((8, 256), F32)
        for at in places:
            e = jnp.exp2(scores[h, at:at + 128, own] - top)
            scores[h, at:at + 128, own] = e
            total = total + jnp.sum(in_eights(e), axis=0)
        return top, across_lanes(total)

    def toward_center(unit, places):
        h, chip = unit
        own = queries_of(chip)
        center = jnp.zeros((8, 256), F32)
        for at in places:
            row = key_row(chip, at)
            toward = dot(kv[row:row + 128, value_lanes(h)], gc[own, head_of(h)], ((1,), (1,)))
            gradw[h, at:at + 128, own] = toward
            center = center + jnp.sum(in_eights(scores[h, at:at + 128, own] * toward), axis=0)
        return across_lanes(center)

    units = [(h, chip) for chip in range(2) for h in range(HEADS)]
    parts = ((S2, S3), (S4, S5, S6), (S1,))
    tops, totals, sums = ({unit: {} for unit in units} for _ in range(3))

    def add_exponents(unit, n):
        tops[unit][n], totals[unit][n] = exponents(unit, parts[n])

    def add_center(unit, n):
        sums[unit][n] = toward_center(unit, parts[n])

    for unit in units[0:2]:
        add_exponents(unit, 0)
        add_center(unit, 0)
    for copy in in_q:
        copy.wait_recv()
    for unit in units[2:4]:
        add_exponents(unit, 0)
        add_exponents(unit, 2)
    in_stat.wait_recv()
    for copy in in_ga:
        copy.wait_recv()
    for unit in units[2:4]:
        add_center(unit, 0)
        add_center(unit, 2)
    for copy in far:
        copy.wait_recv()
    for unit in units[2:4] + units[0:2]:
        add_exponents(unit, 1)
        add_center(unit, 1)
    for copy in in1:
        copy.wait_recv()
    for unit in units[0:2]:
        add_exponents(unit, 2)
        add_center(unit, 2)

    scales, centers = {}, {}
    for unit in units:
        h, chip = unit
        if chip == 0:
            stat = near_stats[h]
        else:
            stat = tuple(stat_in[3 * h + n:3 * h + n + 1, :] for n in range(3))
        every = [tops[unit][n] for n in range(3)] + [stat[0]]
        masses = [totals[unit][n] for n in range(3)] + [stat[1]]
        weighted = [sums[unit][n] for n in range(3)] + [stat[2]]
        best = functools.reduce(jnp.maximum, every)
        factors = [jnp.exp2(top - best) for top in every]
        inverse = 1.0 / sum(f * mass for f, mass in zip(factors, masses))
        centers[unit] = sum(f * part for f, part in zip(factors, weighted)) * inverse
        scales[unit] = [f * inverse for f in factors]
        if chip == 1:
            final_out[2 * h:2 * h + 1, :] = scales[unit][3]
            final_out[2 * h + 1:2 * h + 2, :] = centers[unit]
    in_final = send(final_out, final_in, z_peer[1][0])

    def normalise(h, chip, n):
        own = queries_of(chip)
        for at in parts[n]:
            weight = scores[h, at:at + 128, own] * scales[h, chip][n]
            prob[h, at:at + 128, own] = weight.astype(BF16)
            dsc[h, at:at + 128, own] = (weight * (gradw[h, at:at + 128, own] - centers[h, chip])).astype(BF16)

    def gradients(h, low, high, own=slice(0, 512)):
        d_key = dot(dsc[h, low:high, own], qc[own, head_of(h)]) * ROOT
        d_value = dot(prob[h, low:high, own], gc[own, head_of(h)])
        return d_key, d_value

    def piece(low, rows):
        return out.at[low:low + rows, :]

    def to_queries(h, chip, lanes, weights):
        own, level1 = queries_of(chip), key_row(chip, S1)
        total = dot(kv[L2:ROWS, lanes], weights[h, S2:KEYS, own], ((0,), (0,)))
        return (total + dot(kv[level1:level1 + 128, lanes], weights[h, S1:S2, own], ((0,), (0,)))).T

    for h in range(HEADS):
        for n in range(3):
            normalise(h, 1, n)
        far_attn[:, head_of(h)] = to_queries(h, 1, value_lanes(h), prob).astype(BF16)
    in_rest_attn = [send(at_pair(far_attn, i), rest_attn.at[i], pair_peer[2 + i]) for i in range(2)]
    for h in range(HEADS):
        far_q[:, head_of(h)] = (to_queries(h, 1, key_lanes(h), dsc) * ROOT).astype(BF16)
    in_rest_q = [send(at_pair(far_q, i), rest_q.at[i], pair_peer[2 + i]) for i in range(2)]

    for h in range(HEADS):
        normalise(h, 0, 1)
        d_key, d_value = gradients(h, S4, KEYS)
        out[S4:KEYS, key_lanes(h)] = d_key.astype(BF16)
        out[S4:KEYS, value_lanes(h)] = d_value.astype(BF16)

    def xy_back(half):
        copies = [send(piece(S4 + 64 * half, 64), back.at[half, 0:64, :], xy_peer[1])]
        for m in range(2, 4):
            at = 64 + 32 * (m - 2)
            copies.append(send(piece(S5 + 64 * (m - 2) + 32 * half, 32), back.at[half, at:at + 32, :], xy_peer[m]))
        for m in range(4, 8):
            at = 128 + 16 * (m - 4)
            copies.append(send(piece(S6 + 32 * (m - 4) + 16 * half, 16), back.at[half, at:at + 16, :], xy_peer[m]))
        return copies

    back_near = xy_back(0)
    back_far = xy_back(1)

    for h in range(HEADS):
        normalise(h, 0, 0)
        normalise(h, 0, 2)
    for h in range(HEADS):
        d_key, d_value = gradients(h, S2, S4)
        out123[128:384, key_lanes(h)] = d_key
        out123[128:384, value_lanes(h)] = d_value
        d_key, d_value = gradients(h, S1, S2, queries_of(0))
        out123[0:128, key_lanes(h)] = d_key
        out123[0:128, value_lanes(h)] = d_value

    double = spread(256, ((2, 128, 1),))
    in_near = []
    for t in range(2):
        if t == 1:
            in_final.wait_recv()
        by, to = (qc, gc) if t == 0 else (qm, gm)
        for h in range(HEADS):
            u = 2 * t + h
            if t == 0:
                scale, center = scales[h, 0][3], centers[h, 0]
            else:
                scale, center = final_in[2 * h:2 * h + 1, :], final_in[2 * h + 1:2 * h + 2, :]
            weight = scores_o[u] * scale
            prob_o[u] = weight.astype(BF16)
            dsc_o[u] = (weight * (gradw_o[u] - center)).astype(BF16)
            for weights, source, beyond, lanes, factor in (
                (dsc_o, by, dsc, key_lanes(h, t), ROOT), (prob_o, to, prob, value_lanes(h, t), 1.0)
            ):
                total = dot(weights[u], source[0:256, head_of(h)])
                if t == 0:
                    level1 = dot(double, beyond[h, S1:S2, 256:512]).astype(BF16)
                    total = total + dot(level1, source[256:512, head_of(h)])
                acc[:, lanes] = total * factor
            attn_part = dot(kvo[:, value_lanes(h, t)], prob_o[u], ((0,), (0,))).T
            q_part = dot(kvo[:, key_lanes(h, t)], dsc_o[u], ((0,), (0,))).T
            if t == 0:
                attn_part = attn_part + to_queries(h, 0, value_lanes(h), prob)
                q_part = q_part + to_queries(h, 0, key_lanes(h), dsc)
            near_attn[t, :, head_of(h)] = attn_part.astype(BF16)
            near_q[t, :, head_of(h)] = (q_part * ROOT).astype(BF16)
        if t == 0:
            in_near += [send(near_attn.at[0, 128:256, :], whole.at[:, cols(0)], other)]
            in_near += [send(near_q.at[0, 128:256, :], grad_q.at[:, cols(0)], other)]
        else:
            in_near += [send(near_attn.at[1, 128:256, :], rest_attn.at[2], other)]
            in_near += [send(near_q.at[1, 128:256, :], rest_q.at[2], other)]

    for copy in back_near:
        copy.wait_recv()
    g4 = dot(spread(64, ((1, 64, 1), (2, 32, 2), (4, 16, 4))), back[0]).astype(BF16)
    out[0:128, :] = (out123[0:128, :] + dot(spread(128, ((8, 16, 1),)), g4[16:32])).astype(BF16)
    out[128:256, :] = (out123[128:256, :] + dot(spread(128, ((4, 32, 1),)), g4[32:64])).astype(BF16)
    home = [send(piece(S1 + 64 * sub, 64), zin.at[2 + sub, 0:64, :], z_peer[1][sub]) for sub in range(2)]
    home += [
        send(piece(S2 + (2 * i + sub) * 32, 32), zin.at[2 * (m % 2) + sub, 64:96, :], z_peer[m][sub])
        for i, m in enumerate((2, 3))
        for sub in range(2)
    ]
    acc[:, 0:LANES] += dot(spread(256, ((16, 16, 1),)), g4[0:16])
    home += [send(acc.at[128:256, :], acc_core, other)]

    whole[:, cols(0)] = near_attn[0, 0:128, :]
    grad_q[:, cols(0)] = near_q[0, 0:128, :]
    for copy in in_near + in_rest_attn:
        copy.wait_recv()
    whole[:, cols(2)] = (near_attn[1, 0:128, :].astype(F32) + rest_attn[0].astype(F32)).astype(BF16)
    whole[:, cols(3)] = (rest_attn[2].astype(F32) + rest_attn[1].astype(F32)).astype(BF16)
    send_part[...] = dot(whole[...], w[:, far_cols]).astype(BF16)
    part = send(send_part, recv_part, across)
    for copy in back_far:
        copy.wait_recv()
    mix = spread(128, ((2, 64, 1), (4, 32, 2), (8, 16, 4)))
    out[S3:S4, :] = (out123[256:384, :] + dot(mix, back[1])).astype(BF16)
    home += [
        send(
            piece(S3 + (2 * i + sub) * 16, 16),
            zin.at[2 * (m % 2) + sub, 96 + 16 * (i // 2):112 + 16 * (i // 2), :],
            z_peer[m][sub],
        )
        for i, m in enumerate((4, 5, 6, 7))
        for sub in range(2)
    ]

    for copy in in_rest_q:
        copy.wait_recv()
    grad_q[:, cols(2)] = (near_q[1, 0:128, :].astype(F32) + rest_q[0].astype(F32)).astype(BF16)
    grad_q[:, cols(3)] = (rest_q[2].astype(F32) + rest_q[1].astype(F32)).astype(BF16)
    own_part = dot(whole[...], w[:, my_cols])
    part.wait_recv()
    layer_out[...] = (own_part + recv_part[...].astype(F32)).astype(BF16)

    mix = spread(128, ((2, 64, 1), (4, 32, 1), (8, 16, 2)))
    for copy in home:
        copy.wait_recv()
    bases = (acc[0:128, 0:LANES], acc_core[:, 0:LANES], acc[0:128, LANES:1024], acc_core[:, LANES:1024])
    for j, base in enumerate(bases):
        low = 64 if j < 2 else 0
        total = (base + dot(mix[:, low:128], zin[j, low:128, :])).astype(BF16)
        grad_k[:, cols(j)] = total[:, 0:QUARTER]
        grad_v[:, cols(j)] = total[:, QUARTER:LANES]
    for copy in started:
        copy.wait_send()


COPIES = 96


def store(*refs):
    sems = refs[8]
    copies = [pltpu.make_async_copy(refs[i], refs[4 + i], sems.at[i]) for i in range(4)]
    for copy in copies:
        copy.start()
    for copy in copies:
        copy.wait()


def local(queries, key_vectors, value_vectors, slopes, w_out, grad_out):
    block = jax.ShapeDtypeStruct((B, 1024), BF16)
    vmem = pl.BlockSpec(memory_space=pltpu.VMEM)
    hbm = pl.BlockSpec(memory_space=pltpu.HBM)
    arguments = (slopes, queries, key_vectors, value_vectors, grad_out, w_out)
    results = pl.pallas_call(
        kernel,
        out_shape=[pltpu.VMEM((B, 1024), BF16)] * 4,
        in_specs=[hbm] * 6,
        out_specs=[vmem] * 4,
        scratch_shapes=[
            pltpu.SMEM((8,), F32),
            pltpu.VMEM((ROWS, LANES), BF16),
            pltpu.VMEM((256, 1024), BF16),
            pltpu.VMEM((128, 1024), BF16),
            pltpu.VMEM((512, QUARTER), BF16),
            pltpu.VMEM((256, QUARTER), BF16),
            pltpu.VMEM((512, QUARTER), BF16),
            pltpu.VMEM((256, QUARTER), BF16),
            pltpu.VMEM((128, 1024), BF16),
            pltpu.VMEM((128, 1024), BF16),
            pltpu.VMEM((1024, 2048), BF16),
            pltpu.VMEM((4, 64, LANES), BF16),
            pltpu.VMEM((4, 32, LANES), BF16),
            pltpu.VMEM((4, 16, LANES), BF16),
            pltpu.VMEM((32, LANES), BF16),
            pltpu.VMEM((128, LANES), BF16),
            pltpu.VMEM((64, LANES), BF16),
            pltpu.VMEM((32, LANES), BF16),
            pltpu.VMEM((HEADS, KEYS, 512), F32),
            pltpu.VMEM((HEADS, KEYS, 512), F32),
            pltpu.VMEM((HEADS, KEYS, 512), BF16),
            pltpu.VMEM((HEADS, KEYS, 512), BF16),
            pltpu.VMEM((4, 256, 256), F32),
            pltpu.VMEM((4, 256, 256), F32),
            pltpu.VMEM((4, 256, 256), BF16),
            pltpu.VMEM((4, 256, 256), BF16),
            pltpu.VMEM((8, 256), F32),
            pltpu.VMEM((8, 256), F32),
            pltpu.VMEM((8, 256), F32),
            pltpu.VMEM((8, 256), F32),
            pltpu.VMEM((KEYS, LANES), BF16),
            pltpu.VMEM((384, LANES), F32),
            pltpu.VMEM((2, 192, LANES), BF16),
            pltpu.VMEM((4, 128, LANES), BF16),
            pltpu.VMEM((256, 1024), F32),
            pltpu.VMEM((128, 1024), F32),
            pltpu.VMEM((256, QUARTER), BF16),
            pltpu.VMEM((256, QUARTER), BF16),
            pltpu.VMEM((2, 256, QUARTER), BF16),
            pltpu.VMEM((2, 256, QUARTER), BF16),
            pltpu.VMEM((3, 128, QUARTER), BF16),
            pltpu.VMEM((3, 128, QUARTER), BF16),
            pltpu.VMEM((128, 1024), BF16),
            pltpu.VMEM((128, 1024), BF16),
            pltpu.VMEM((128, 1024), BF16),
            pltpu.VMEM((128, 1024), BF16),
            pltpu.SemaphoreType.DMA((COPIES,)),
            pltpu.SemaphoreType.DMA((COPIES,)),
            pltpu.SemaphoreType.DMA((13,)),
        ],
        compiler_params=pltpu.CompilerParams(
            collective_id=0, has_side_effects=True, vmem_limit_bytes=48 * 1024 * 1024
        ),
        cost_estimate=pl.CostEstimate(flops=2_700_000_000, bytes_accessed=8_000_000, transcendentals=1_000_000),
    )(*(pltpu.with_memory_space_constraint(x, pltpu.HBM) for x in arguments))
    return pl.pallas_call(
        store,
        out_shape=[block] * 4,
        in_specs=[vmem] * 4,
        out_specs=[hbm] * 4,
        scratch_shapes=[pltpu.SemaphoreType.DMA((4,))],
    )(*(pltpu.with_memory_space_constraint(x, pltpu.VMEM) for x in results))


def solution(mesh):
    cut = P("ctx", "head")
    return jax.shard_map(
        local,
        mesh=mesh,
        in_specs=(cut, cut, cut, P("head"), P("head", None), cut),
        out_specs=(cut, cut, cut, cut),
        check_vma=False,
    )
```

```python
import functools
import math

import jax
import jax.numpy as jnp
from jax import lax
from jax.experimental import pallas as pl
from jax.experimental.pallas import tpu as pltpu
from jax.sharding import PartitionSpec as P

B = 128
HEAD = 128
HEADS = 2
QUARTER = 256
LANES = 512
LOG_TWO = math.log(2.0)
LOG2E = 1.0 / LOG_TWO
ROOT = 1.0 / math.sqrt(HEAD)
F32 = jnp.float32
BF16 = jnp.bfloat16
MESH = pl.DeviceIdType.MESH

L1, OWN1, L2, L3, L4, L5, L6, ROWS = 0, 128, 256, 384, 512, 640, 768, 896
S1, S2, S3, S4, S5, S6, KEYS = 0, 128, 256, 384, 512, 640, 768


def flip(index, bits):
    out = index
    for bit in bits:
        side = (index // (1 << bit)) % 2
        out = out + (1 - 2 * side) * (1 << bit)
    return out


def bits_of(mask, first):
    return [first + i for i in range(3) if mask >> i & 1]


def dot(a, b, dims=((1,), (0,))):
    return lax.dot_general(a, b, (dims, ((), ())), preferred_element_type=F32)


def grid_of(rows, columns):
    r = lax.broadcasted_iota(jnp.int32, (rows, columns), 0)
    c = lax.broadcasted_iota(jnp.int32, (rows, columns), 1)
    return r, c


def pools(rows, ratios):
    blocks = []
    for ratio in ratios:
        r, c = grid_of(rows // ratio, rows)
        blocks.append(jnp.where(c // ratio == r, 1.0 / ratio, 0.0).astype(BF16))
    return jnp.concatenate(blocks, axis=0)


def spread(rows, parts):
    blocks = []
    for ratio, width, copies in parts:
        r, c = grid_of(rows, width * copies)
        blocks.append(jnp.where(r // ratio == c % width, 1.0 / ratio, 0.0).astype(BF16))
    return jnp.concatenate(blocks, axis=1)


def in_eights(x):
    return x.reshape(x.shape[0] // 8, 8, x.shape[1])


def kernel(
    slopes_in, q, k, v, g, w_in,
    layer_out, grad_q, grad_k, grad_v,
    slopes, kv, kvo, kt, qc, qm, gc, gm, gown, gfar, w, s1, s2, s3, mate3, a4, a5, a6,
    scores, gradw, prob, dsc, scores_o, gradw_o, prob_o, dsc_o, stat_out, stat_in, final_out, final_in,
    out, out123, back, zin, acc, acc_core,
    far_q, far_attn, near_q, near_attn, rest_q, rest_attn, whole, ga, send_part, recv_part,
    send_sem, recv_sem, local_sem,
):
    ctx = lax.axis_index("ctx")
    head = lax.axis_index("head")
    core = ctx % 2
    place = (ctx // 2) % 2

    def cols(j):
        a, c = j // 2, j % 2
        number = (place + a - 2 * place * a) * 2 + (core + c - 2 * core * c)
        return pl.ds(pl.multiple_of(number * QUARTER, QUARTER), QUARTER)

    my_cols = pl.ds(pl.multiple_of(head * 1024, 1024), 1024)
    far_cols = pl.ds(pl.multiple_of((1 - head) * 1024, 1024), 1024)

    across = (ctx, 1 - head)
    z_peer = [[(flip(ctx, [0] * sub + bits_of(m, 1)), head) for sub in range(2)] for m in range(8)]
    other = z_peer[0][1]
    xy_peer = [None] + [(flip(ctx, bits_of(m, 4)), head) for m in range(1, 8)]

    def load(src, dst, slot):
        copy = pltpu.make_async_copy(src, dst, local_sem.at[slot])
        copy.start()
        return copy

    load_kv = []
    for j in range(4):
        into, at = (kvo, 0) if j % 2 == 0 else (kt, 0)
        left = LANES * (j // 2)
        load_kv.append(load(k.at[:, cols(j)], into.at[0:128, left:left + QUARTER], 2 * j))
        load_kv.append(load(v.at[:, cols(j)], into.at[0:128, left + QUARTER:left + LANES], 2 * j + 1))

    barrier = pltpu.get_barrier_semaphore()
    peers = [other, across] + sum(z_peer[1:], []) + xy_peer[1:]
    for peer in peers:
        pl.semaphore_signal(barrier, inc=1, device_id=peer, device_id_type=MESH)

    load_rest = [
        load(q.at[:, cols(0)], qc.at[0:128, :], 8),
        load(q.at[:, cols(2)], qm.at[0:128, :], 9),
        load(g, gown, 10),
        load(slopes_in, slopes, 11),
    ]
    stat_out[...] = jnp.zeros_like(stat_out)
    final_out[...] = jnp.zeros_like(final_out)
    for copy in load_kv:
        copy.wait()
    load_rest.append(load(w_in, w, 12))
    means = pools(128, (2, 4, 8))
    for j in range(4):
        left = LANES * (j // 2)
        pooled = dot(means, kvo[0:128, left:left + LANES] if j % 2 == 0 else kt[:, left:left + LANES]).astype(BF16)
        s1[j] = pooled[0:64]
        s2[j] = pooled[64:96]
        s3[j] = pooled[96:112]

    pl.semaphore_wait(barrier, len(peers))

    count = [0]
    started = []

    def send(src, dst, peer):
        slot = count[0]
        count[0] += 1
        copy = pltpu.make_async_remote_copy(
            src_ref=src, dst_ref=dst, send_sem=send_sem.at[slot], recv_sem=recv_sem.at[slot],
            device_id=peer, device_id_type=MESH,
        )
        copy.start()
        started.append(copy)
        return copy

    pair_peer = [None, other, z_peer[1][0], z_peer[1][1]]

    def at_pair(ref, j):
        return ref.at[128 * j:128 * j + 128, :]

    def z_sends(source, low, rows, masks):
        return [
            send(
                source.at[2 * (m % 2) + sub],
                kv.at[low + (2 * i + sub) * rows:low + (2 * i + sub + 1) * rows, :],
                z_peer[m][sub],
            )
            for i, m in enumerate(masks)
            for sub in range(2)
        ]

    in3 = z_sends(s3, L3, 16, (4, 5, 6, 7))
    in_mate = [send(s3.at[2 + sub], mate3.at[16 * sub:16 * sub + 16, :], z_peer[1][sub]) for sub in range(2)]
    in2 = z_sends(s2, L2, 32, (2, 3))
    in1 = z_sends(s1, L1, 64, (1,))
    in_kv = send(kt, kvo.at[128:256, :], other)
    in_g = send(g, gfar, across)
    in_q_core = [send(q.at[:, cols(1)], at_pair(qc, 1), other), send(q.at[:, cols(3)], at_pair(qm, 1), other)]
    in_q = [send(q.at[:, cols(j)], at_pair(qc, j), pair_peer[j]) for j in range(2, 4)]

    in_kv.wait_recv()
    kv[OWN1:L2, :] = dot(pools(256, (2,)), kvo[:, 0:LANES]).astype(BF16)
    a4[0:16, :] = dot(pools(256, (16,)), kvo[:, 0:LANES]).astype(BF16)

    def xy_sends(half):
        copies = [send(a4.at[64 * half:64 * half + 64, :], kv.at[L4 + 64 * half:L4 + 64 * half + 64, :], xy_peer[1])]
        for m in range(2, 4):
            low = L5 + 64 * (m - 2) + 32 * half
            copies.append(send(a5.at[32 * half:32 * half + 32, :], kv.at[low:low + 32, :], xy_peer[m]))
        for m in range(4, 8):
            low = L6 + 32 * (m - 4) + 16 * half
            copies.append(send(a6.at[16 * half:16 * half + 16, :], kv.at[low:low + 16, :], xy_peer[m]))
        return copies

    for copy in in3:
        copy.wait_recv()
    upper = dot(pools(128, (2, 4, 8)), kv[L3:L4, :]).astype(BF16)
    a4[64:128, :] = upper[0:64]
    a5[32:64, :] = upper[64:96]
    a6[16:32, :] = upper[96:112]
    far = xy_sends(1)

    for copy in load_rest:
        copy.wait()
    in_g.wait_recv()
    ga[...] = (
        dot(gown[...], w[:, my_cols], ((1,), (1,))) + dot(gfar[...], w[:, far_cols], ((1,), (1,)))
    ).astype(BF16)
    in_ga = [send(ga.at[:, cols(j)], at_pair(gc, j), pair_peer[j]) for j in range(2, 4)]
    in_ga_core = [send(ga.at[:, cols(1)], at_pair(gc, 1), other), send(ga.at[:, cols(3)], at_pair(gm, 1), other)]
    gc[0:128, :] = ga[:, cols(0)]
    gm[0:128, :] = ga[:, cols(2)]

    lane = lax.broadcasted_iota(jnp.int32, (1, 256), 1)

    def level_bias(t, h, level):
        slope = slopes[((place + t - 2 * place * t) * 2 + core) * HEADS + h]
        return (level * LOG_TWO - slope * (level + 1.0)) * LOG2E

    def key_lanes(h, t=0):
        return slice(LANES * t + h * HEAD, LANES * t + (h + 1) * HEAD)

    def value_lanes(h, t=0):
        return slice(LANES * t + QUARTER + h * HEAD, LANES * t + QUARTER + (h + 1) * HEAD)

    def queries_of(chip):
        return slice(256 * chip, 256 * chip + 256)

    def head_of(h):
        return slice(h * HEAD, (h + 1) * HEAD)

    def across_lanes(x):
        return jnp.sum(x, axis=0, keepdims=True)

    def own_stats(t, h):
        by, to = (qc, gc) if t == 0 else (qm, gm)
        u = 2 * t + h
        tops = []
        for at in (0, 128):
            rows = slice(at, at + 128)
            bias = jnp.where((lane < 128) == (at == 0), 0.0, level_bias(t, h, 0))
            s = dot(kvo[rows, key_lanes(h, t)], by[0:256, head_of(h)], ((1,), (1,))) * (ROOT * LOG2E) + bias
            scores_o[u, rows, :] = s
            tops.append(jnp.max(in_eights(s), axis=0))
        top = jnp.max(jnp.maximum(tops[0], tops[1]), axis=0, keepdims=True)
        total = jnp.zeros((8, 256), F32)
        center = jnp.zeros((8, 256), F32)
        for at in (0, 128):
            rows = slice(at, at + 128)
            e = jnp.exp2(scores_o[u, rows, :] - top)
            scores_o[u, rows, :] = e
            toward = dot(kvo[rows, value_lanes(h, t)], to[0:256, head_of(h)], ((1,), (1,)))
            gradw_o[u, rows, :] = toward
            total = total + jnp.sum(in_eights(e), axis=0)
            center = center + jnp.sum(in_eights(e * toward), axis=0)
        return top, across_lanes(total), across_lanes(center)

    for copy in in_mate + in2:
        copy.wait_recv()
    a4[16:32, :] = dot(pools(32, (2,)), mate3[...]).astype(BF16)
    a4[32:64, :] = dot(pools(128, (4,)), kv[L2:L3, :]).astype(BF16)
    upper = dot(pools(64, (2, 4)), a4[0:64, :]).astype(BF16)
    a5[0:32, :] = upper[0:32]
    a6[0:16, :] = upper[32:48]
    far += xy_sends(0)

    for copy in in_q_core + in_ga_core:
        copy.wait_recv()
    near_stats = [own_stats(0, h) for h in range(HEADS)]

    for h in range(HEADS):
        for n, stat in enumerate(own_stats(1, h)):
            stat_out[3 * h + n:3 * h + n + 1, :] = stat
    in_stat = send(stat_out, stat_in, z_peer[1][0])

    def key_row(chip, at):
        return L1 + 128 * chip if at == S1 else L2 + at - S2

    def exponents(unit, places):
        h, chip = unit
        own = queries_of(chip)
        tops = []
        for at in places:
            row = key_row(chip, at)
            s = dot(kv[row:row + 128, key_lanes(h)], qc[own, head_of(h)], ((1,), (1,))) * (ROOT * LOG2E)
            s = s + level_bias(0, h, at // 128 + 1)
            scores[h, at:at + 128, own] = s
            tops.append(jnp.max(in_eights(s), axis=0))
        top = jnp.max(functools.reduce(jnp.maximum, tops), axis=0, keepdims=True)
        total = jnp.zeros((8, 256), F32)
        for at in places:
            e = jnp.exp2(scores[h, at:at + 128, own] - top)
            scores[h, at:at + 128, own] = e
            total = total + jnp.sum(in_eights(e), axis=0)
        return top, across_lanes(total)

    def toward_center(unit, places):
        h, chip = unit
        own = queries_of(chip)
        center = jnp.zeros((8, 256), F32)
        for at in places:
            row = key_row(chip, at)
            toward = dot(kv[row:row + 128, value_lanes(h)], gc[own, head_of(h)], ((1,), (1,)))
            gradw[h, at:at + 128, own] = toward
            center = center + jnp.sum(in_eights(scores[h, at:at + 128, own] * toward), axis=0)
        return across_lanes(center)

    units = [(h, chip) for chip in range(2) for h in range(HEADS)]
    parts = ((S2, S3), (S4, S5, S6), (S1,))
    tops, totals, sums = ({unit: {} for unit in units} for _ in range(3))

    def add_exponents(unit, n):
        tops[unit][n], totals[unit][n] = exponents(unit, parts[n])

    def add_center(unit, n):
        sums[unit][n] = toward_center(unit, parts[n])

    for unit in units[0:2]:
        add_exponents(unit, 0)
        add_center(unit, 0)
    for copy in in_q:
        copy.wait_recv()
    for unit in units[2:4]:
        add_exponents(unit, 0)
        add_exponents(unit, 2)
    in_stat.wait_recv()
    for copy in in_ga:
        copy.wait_recv()
    for unit in units[2:4]:
        add_center(unit, 0)
        add_center(unit, 2)
    for copy in far:
        copy.wait_recv()
    for unit in units[2:4] + units[0:2]:
        add_exponents(unit, 1)
        add_center(unit, 1)
    for copy in in1:
        copy.wait_recv()
    for unit in units[0:2]:
        add_exponents(unit, 2)
        add_center(unit, 2)

    scales, centers = {}, {}
    for unit in units:
        h, chip = unit
        if chip == 0:
            stat = near_stats[h]
        else:
            stat = tuple(stat_in[3 * h + n:3 * h + n + 1, :] for n in range(3))
        every = [tops[unit][n] for n in range(3)] + [stat[0]]
        masses = [totals[unit][n] for n in range(3)] + [stat[1]]
        weighted = [sums[unit][n] for n in range(3)] + [stat[2]]
        best = functools.reduce(jnp.maximum, every)
        factors = [jnp.exp2(top - best) for top in every]
        inverse = 1.0 / sum(f * mass for f, mass in zip(factors, masses))
        centers[unit] = sum(f * part for f, part in zip(factors, weighted)) * inverse
        scales[unit] = [f * inverse for f in factors]
        if chip == 1:
            final_out[2 * h:2 * h + 1, :] = scales[unit][3]
            final_out[2 * h + 1:2 * h + 2, :] = centers[unit]
    in_final = send(final_out, final_in, z_peer[1][0])

    def normalise(h, chip, n):
        own = queries_of(chip)
        for at in parts[n]:
            weight = scores[h, at:at + 128, own] * scales[h, chip][n]
            prob[h, at:at + 128, own] = weight.astype(BF16)
            dsc[h, at:at + 128, own] = (weight * (gradw[h, at:at + 128, own] - centers[h, chip])).astype(BF16)

    def gradients(h, low, high, own=slice(0, 512)):
        d_key = dot(dsc[h, low:high, own], qc[own, head_of(h)]) * ROOT
        d_value = dot(prob[h, low:high, own], gc[own, head_of(h)])
        return d_key, d_value

    def piece(low, rows):
        return out.at[low:low + rows, :]

    def to_queries(h, chip, lanes, weights):
        own, level1 = queries_of(chip), key_row(chip, S1)
        total = dot(kv[L2:ROWS, lanes], weights[h, S2:KEYS, own], ((0,), (0,)))
        return (total + dot(kv[level1:level1 + 128, lanes], weights[h, S1:S2, own], ((0,), (0,)))).T

    for h in range(HEADS):
        for n in range(3):
            normalise(h, 1, n)
        far_attn[:, head_of(h)] = to_queries(h, 1, value_lanes(h), prob).astype(BF16)
    in_rest_attn = [send(at_pair(far_attn, i), rest_attn.at[i], pair_peer[2 + i]) for i in range(2)]
    for h in range(HEADS):
        far_q[:, head_of(h)] = (to_queries(h, 1, key_lanes(h), dsc) * ROOT).astype(BF16)
    in_rest_q = [send(at_pair(far_q, i), rest_q.at[i], pair_peer[2 + i]) for i in range(2)]

    for h in range(HEADS):
        normalise(h, 0, 1)
        d_key, d_value = gradients(h, S4, KEYS)
        out[S4:KEYS, key_lanes(h)] = d_key.astype(BF16)
        out[S4:KEYS, value_lanes(h)] = d_value.astype(BF16)

    def xy_back(half):
        copies = [send(piece(S4 + 64 * half, 64), back.at[half, 0:64, :], xy_peer[1])]
        for m in range(2, 4):
            at = 64 + 32 * (m - 2)
            copies.append(send(piece(S5 + 64 * (m - 2) + 32 * half, 32), back.at[half, at:at + 32, :], xy_peer[m]))
        for m in range(4, 8):
            at = 128 + 16 * (m - 4)
            copies.append(send(piece(S6 + 32 * (m - 4) + 16 * half, 16), back.at[half, at:at + 16, :], xy_peer[m]))
        return copies

    back_near = xy_back(0)
    back_far = xy_back(1)

    for h in range(HEADS):
        normalise(h, 0, 0)
        normalise(h, 0, 2)
    for h in range(HEADS):
        d_key, d_value = gradients(h, S2, S4)
        out123[128:384, key_lanes(h)] = d_key
        out123[128:384, value_lanes(h)] = d_value
        d_key, d_value = gradients(h, S1, S2, queries_of(0))
        out123[0:128, key_lanes(h)] = d_key
        out123[0:128, value_lanes(h)] = d_value

    double = spread(256, ((2, 128, 1),))
    in_near = []
    for t in range(2):
        if t == 1:
            in_final.wait_recv()
        by, to = (qc, gc) if t == 0 else (qm, gm)
        for h in range(HEADS):
            u = 2 * t + h
            if t == 0:
                scale, center = scales[h, 0][3], centers[h, 0]
            else:
                scale, center = final_in[2 * h:2 * h + 1, :], final_in[2 * h + 1:2 * h + 2, :]
            weight = scores_o[u] * scale
            prob_o[u] = weight.astype(BF16)
            dsc_o[u] = (weight * (gradw_o[u] - center)).astype(BF16)
            for weights, source, beyond, lanes, factor in (
                (dsc_o, by, dsc, key_lanes(h, t), ROOT), (prob_o, to, prob, value_lanes(h, t), 1.0)
            ):
                total = dot(weights[u], source[0:256, head_of(h)])
                if t == 0:
                    level1 = dot(double, beyond[h, S1:S2, 256:512]).astype(BF16)
                    total = total + dot(level1, source[256:512, head_of(h)])
                acc[:, lanes] = total * factor
            attn_part = dot(kvo[:, value_lanes(h, t)], prob_o[u], ((0,), (0,))).T
            q_part = dot(kvo[:, key_lanes(h, t)], dsc_o[u], ((0,), (0,))).T
            if t == 0:
                attn_part = attn_part + to_queries(h, 0, value_lanes(h), prob)
                q_part = q_part + to_queries(h, 0, key_lanes(h), dsc)
            near_attn[t, :, head_of(h)] = attn_part.astype(BF16)
            near_q[t, :, head_of(h)] = (q_part * ROOT).astype(BF16)
        if t == 0:
            in_near += [send(near_attn.at[0, 128:256, :], whole.at[:, cols(0)], other)]
            in_near += [send(near_q.at[0, 128:256, :], grad_q.at[:, cols(0)], other)]
        else:
            in_near += [send(near_attn.at[1, 128:256, :], rest_attn.at[2], other)]
            in_near += [send(near_q.at[1, 128:256, :], rest_q.at[2], other)]

    for copy in back_near:
        copy.wait_recv()
    g4 = dot(spread(64, ((1, 64, 1), (2, 32, 2), (4, 16, 4))), back[0]).astype(BF16)
    out[0:128, :] = (out123[0:128, :] + dot(spread(128, ((8, 16, 1),)), g4[16:32])).astype(BF16)
    out[128:256, :] = (out123[128:256, :] + dot(spread(128, ((4, 32, 1),)), g4[32:64])).astype(BF16)
    home = [
        send(piece(S2 + (2 * i + sub) * 32, 32), zin.at[2 * (m % 2) + sub, 64:96, :], z_peer[m][sub])
        for i, m in enumerate((2, 3))
        for sub in range(2)
    ]
    home += [send(piece(S1 + 64 * 0, 64), zin.at[2 + 0, 0:64, :], z_peer[1][0])]
    home += [send(piece(S1 + 64 * 1, 64), zin.at[2 + 1, 0:64, :], z_peer[1][1])]
    acc[:, 0:LANES] += dot(spread(256, ((16, 16, 1),)), g4[0:16])
    home += [send(acc.at[128:256, :], acc_core, other)]

    whole[:, cols(0)] = near_attn[0, 0:128, :]
    grad_q[:, cols(0)] = near_q[0, 0:128, :]
    for copy in in_near + in_rest_attn:
        copy.wait_recv()
    whole[:, cols(2)] = (near_attn[1, 0:128, :].astype(F32) + rest_attn[0].astype(F32)).astype(BF16)
    whole[:, cols(3)] = (rest_attn[2].astype(F32) + rest_attn[1].astype(F32)).astype(BF16)
    send_part[...] = dot(whole[...], w[:, far_cols]).astype(BF16)
    part = send(send_part, recv_part, across)
    for copy in back_far:
        copy.wait_recv()
    mix = spread(128, ((2, 64, 1), (4, 32, 2), (8, 16, 4)))
    out[S3:S4, :] = (out123[256:384, :] + dot(mix, back[1])).astype(BF16)
    home += [
        send(
            piece(S3 + (2 * i + sub) * 16, 16),
            zin.at[2 * (m % 2) + sub, 96 + 16 * (i // 2):112 + 16 * (i // 2), :],
            z_peer[m][sub],
        )
        for i, m in enumerate((4, 5, 6, 7))
        for sub in range(2)
    ]

    for copy in in_rest_q:
        copy.wait_recv()
    grad_q[:, cols(2)] = (near_q[1, 0:128, :].astype(F32) + rest_q[0].astype(F32)).astype(BF16)
    grad_q[:, cols(3)] = (rest_q[2].astype(F32) + rest_q[1].astype(F32)).astype(BF16)
    own_part = dot(whole[...], w[:, my_cols])
    part.wait_recv()
    layer_out[...] = (own_part + recv_part[...].astype(F32)).astype(BF16)

    mix = spread(128, ((2, 64, 1), (4, 32, 1), (8, 16, 2)))
    for copy in home:
        copy.wait_recv()
    bases = (acc[0:128, 0:LANES], acc_core[:, 0:LANES], acc[0:128, LANES:1024], acc_core[:, LANES:1024])
    for j, base in enumerate(bases):
        low = 64 if j < 2 else 0
        total = (base + dot(mix[:, low:128], zin[j, low:128, :])).astype(BF16)
        grad_k[:, cols(j)] = total[:, 0:QUARTER]
        grad_v[:, cols(j)] = total[:, QUARTER:LANES]
    for copy in started:
        copy.wait_send()


COPIES = 96


def store(*refs):
    sems = refs[8]
    copies = [pltpu.make_async_copy(refs[i], refs[4 + i], sems.at[i]) for i in range(4)]
    for copy in copies:
        copy.start()
    for copy in copies:
        copy.wait()


def local(queries, key_vectors, value_vectors, slopes, w_out, grad_out):
    block = jax.ShapeDtypeStruct((B, 1024), BF16)
    vmem = pl.BlockSpec(memory_space=pltpu.VMEM)
    hbm = pl.BlockSpec(memory_space=pltpu.HBM)
    arguments = (slopes, queries, key_vectors, value_vectors, grad_out, w_out)
    results = pl.pallas_call(
        kernel,
        out_shape=[pltpu.VMEM((B, 1024), BF16)] * 4,
        in_specs=[hbm] * 6,
        out_specs=[vmem] * 4,
        scratch_shapes=[
            pltpu.SMEM((8,), F32),
            pltpu.VMEM((ROWS, LANES), BF16),
            pltpu.VMEM((256, 1024), BF16),
            pltpu.VMEM((128, 1024), BF16),
            pltpu.VMEM((512, QUARTER), BF16),
            pltpu.VMEM((256, QUARTER), BF16),
            pltpu.VMEM((512, QUARTER), BF16),
            pltpu.VMEM((256, QUARTER), BF16),
            pltpu.VMEM((128, 1024), BF16),
            pltpu.VMEM((128, 1024), BF16),
            pltpu.VMEM((1024, 2048), BF16),
            pltpu.VMEM((4, 64, LANES), BF16),
            pltpu.VMEM((4, 32, LANES), BF16),
            pltpu.VMEM((4, 16, LANES), BF16),
            pltpu.VMEM((32, LANES), BF16),
            pltpu.VMEM((128, LANES), BF16),
            pltpu.VMEM((64, LANES), BF16),
            pltpu.VMEM((32, LANES), BF16),
            pltpu.VMEM((HEADS, KEYS, 512), F32),
            pltpu.VMEM((HEADS, KEYS, 512), F32),
            pltpu.VMEM((HEADS, KEYS, 512), BF16),
            pltpu.VMEM((HEADS, KEYS, 512), BF16),
            pltpu.VMEM((4, 256, 256), F32),
            pltpu.VMEM((4, 256, 256), F32),
            pltpu.VMEM((4, 256, 256), BF16),
            pltpu.VMEM((4, 256, 256), BF16),
            pltpu.VMEM((8, 256), F32),
            pltpu.VMEM((8, 256), F32),
            pltpu.VMEM((8, 256), F32),
            pltpu.VMEM((8, 256), F32),
            pltpu.VMEM((KEYS, LANES), BF16),
            pltpu.VMEM((384, LANES), F32),
            pltpu.VMEM((2, 192, LANES), BF16),
            pltpu.VMEM((4, 128, LANES), BF16),
            pltpu.VMEM((256, 1024), F32),
            pltpu.VMEM((128, 1024), F32),
            pltpu.VMEM((256, QUARTER), BF16),
            pltpu.VMEM((256, QUARTER), BF16),
            pltpu.VMEM((2, 256, QUARTER), BF16),
            pltpu.VMEM((2, 256, QUARTER), BF16),
            pltpu.VMEM((3, 128, QUARTER), BF16),
            pltpu.VMEM((3, 128, QUARTER), BF16),
            pltpu.VMEM((128, 1024), BF16),
            pltpu.VMEM((128, 1024), BF16),
            pltpu.VMEM((128, 1024), BF16),
            pltpu.VMEM((128, 1024), BF16),
            pltpu.SemaphoreType.DMA((COPIES,)),
            pltpu.SemaphoreType.DMA((COPIES,)),
            pltpu.SemaphoreType.DMA((13,)),
        ],
        compiler_params=pltpu.CompilerParams(
            collective_id=0, has_side_effects=True, vmem_limit_bytes=48 * 1024 * 1024
        ),
        cost_estimate=pl.CostEstimate(flops=2_700_000_000, bytes_accessed=8_000_000, transcendentals=1_000_000),
    )(*(pltpu.with_memory_space_constraint(x, pltpu.HBM) for x in arguments))
    return pl.pallas_call(
        store,
        out_shape=[block] * 4,
        in_specs=[vmem] * 4,
        out_specs=[hbm] * 4,
        scratch_shapes=[pltpu.SemaphoreType.DMA((4,))],
    )(*(pltpu.with_memory_space_constraint(x, pltpu.VMEM) for x in results))


def solution(mesh):
    cut = P("ctx", "head")
    return jax.shard_map(
        local,
        mesh=mesh,
        in_specs=(cut, cut, cut, P("head"), P("head", None), cut),
        out_specs=(cut, cut, cut, cut),
        check_vma=False,
    )
```

```python
import functools
import math

import jax
import jax.numpy as jnp
from jax import lax
from jax.experimental import pallas as pl
from jax.experimental.pallas import tpu as pltpu
from jax.sharding import PartitionSpec as P

B = 128
HEAD = 128
HEADS = 2
QUARTER = 256
LANES = 512
LOG_TWO = math.log(2.0)
LOG2E = 1.0 / LOG_TWO
ROOT = 1.0 / math.sqrt(HEAD)
F32 = jnp.float32
BF16 = jnp.bfloat16
MESH = pl.DeviceIdType.MESH

L1, OWN1, L2, L3, L4, L5, L6, ROWS = 0, 128, 256, 384, 512, 640, 768, 896
S1, S2, S3, S4, S5, S6, KEYS = 0, 128, 256, 384, 512, 640, 768


def flip(index, bits):
    out = index
    for bit in bits:
        side = (index // (1 << bit)) % 2
        out = out + (1 - 2 * side) * (1 << bit)
    return out


def bits_of(mask, first):
    return [first + i for i in range(3) if mask >> i & 1]


def dot(a, b, dims=((1,), (0,))):
    return lax.dot_general(a, b, (dims, ((), ())), preferred_element_type=F32)


def grid_of(rows, columns):
    r = lax.broadcasted_iota(jnp.int32, (rows, columns), 0)
    c = lax.broadcasted_iota(jnp.int32, (rows, columns), 1)
    return r, c


def pools(rows, ratios):
    blocks = []
    for ratio in ratios:
        r, c = grid_of(rows // ratio, rows)
        blocks.append(jnp.where(c // ratio == r, 1.0 / ratio, 0.0).astype(BF16))
    return jnp.concatenate(blocks, axis=0)


def spread(rows, parts):
    blocks = []
    for ratio, width, copies in parts:
        r, c = grid_of(rows, width * copies)
        blocks.append(jnp.where(r // ratio == c % width, 1.0 / ratio, 0.0).astype(BF16))
    return jnp.concatenate(blocks, axis=1)


def in_eights(x):
    return x.reshape(x.shape[0] // 8, 8, x.shape[1])


def kernel(
    slopes_in, q, k, v, g, w_in,
    layer_out, grad_q, grad_k, grad_v,
    slopes, kv, kvo, kt, qc, qm, gc, gm, gown, gfar, w, s1, s2, s3, mate3, a4, a5, a6,
    scores, gradw, prob, dsc, scores_o, gradw_o, prob_o, dsc_o, stat_out, stat_in, final_out, final_in,
    out, out123, back, zin, acc, acc_core, early,
    far_q, far_attn, near_q, near_attn, rest_q, rest_attn, whole, ga, send_part, recv_part,
    send_sem, recv_sem, local_sem,
):
    ctx = lax.axis_index("ctx")
    head = lax.axis_index("head")
    core = ctx % 2
    place = (ctx // 2) % 2

    def cols(j):
        a, c = j // 2, j % 2
        number = (place + a - 2 * place * a) * 2 + (core + c - 2 * core * c)
        return pl.ds(pl.multiple_of(number * QUARTER, QUARTER), QUARTER)

    my_cols = pl.ds(pl.multiple_of(head * 1024, 1024), 1024)
    far_cols = pl.ds(pl.multiple_of((1 - head) * 1024, 1024), 1024)

    across = (ctx, 1 - head)
    z_peer = [[(flip(ctx, [0] * sub + bits_of(m, 1)), head) for sub in range(2)] for m in range(8)]
    other = z_peer[0][1]
    xy_peer = [None] + [(flip(ctx, bits_of(m, 4)), head) for m in range(1, 8)]

    def load(src, dst, slot):
        copy = pltpu.make_async_copy(src, dst, local_sem.at[slot])
        copy.start()
        return copy

    load_kv = []
    for j in range(4):
        into, at = (kvo, 0) if j % 2 == 0 else (kt, 0)
        left = LANES * (j // 2)
        load_kv.append(load(k.at[:, cols(j)], into.at[0:128, left:left + QUARTER], 2 * j))
        load_kv.append(load(v.at[:, cols(j)], into.at[0:128, left + QUARTER:left + LANES], 2 * j + 1))

    barrier = pltpu.get_barrier_semaphore()
    peers = [other, across] + sum(z_peer[1:], []) + xy_peer[1:]
    for peer in peers:
        pl.semaphore_signal(barrier, inc=1, device_id=peer, device_id_type=MESH)

    load_rest = [
        load(q.at[:, cols(0)], qc.at[0:128, :], 8),
        load(q.at[:, cols(2)], qm.at[0:128, :], 9),
        load(g, gown, 10),
        load(slopes_in, slopes, 11),
    ]
    stat_out[...] = jnp.zeros_like(stat_out)
    final_out[...] = jnp.zeros_like(final_out)
    for copy in load_kv:
        copy.wait()
    load_rest.append(load(w_in, w, 12))
    means = pools(128, (2, 4, 8))
    for j in range(4):
        left = LANES * (j // 2)
        pooled = dot(means, kvo[0:128, left:left + LANES] if j % 2 == 0 else kt[:, left:left + LANES]).astype(BF16)
        s1[j] = pooled[0:64]
        s2[j] = pooled[64:96]
        s3[j] = pooled[96:112]

    pl.semaphore_wait(barrier, len(peers))

    count = [0]
    started = []

    def send(src, dst, peer):
        slot = count[0]
        count[0] += 1
        copy = pltpu.make_async_remote_copy(
            src_ref=src, dst_ref=dst, send_sem=send_sem.at[slot], recv_sem=recv_sem.at[slot],
            device_id=peer, device_id_type=MESH,
        )
        copy.start()
        started.append(copy)
        return copy

    pair_peer = [None, other, z_peer[1][0], z_peer[1][1]]

    def at_pair(ref, j):
        return ref.at[128 * j:128 * j + 128, :]

    def z_sends(source, low, rows, masks):
        return [
            send(
                source.at[2 * (m % 2) + sub],
                kv.at[low + (2 * i + sub) * rows:low + (2 * i + sub + 1) * rows, :],
                z_peer[m][sub],
            )
            for i, m in enumerate(masks)
            for sub in range(2)
        ]

    in3 = z_sends(s3, L3, 16, (4, 5, 6, 7))
    in_mate = [send(s3.at[2 + sub], mate3.at[16 * sub:16 * sub + 16, :], z_peer[1][sub]) for sub in range(2)]
    in2 = z_sends(s2, L2, 32, (2, 3))
    in1 = z_sends(s1, L1, 64, (1,))
    in_kv = send(kt, kvo.at[128:256, :], other)
    in_g = send(g, gfar, across)
    in_q_core = [send(q.at[:, cols(1)], at_pair(qc, 1), other), send(q.at[:, cols(3)], at_pair(qm, 1), other)]
    in_q = [send(q.at[:, cols(j)], at_pair(qc, j), pair_peer[j]) for j in range(2, 4)]

    in_kv.wait_recv()
    kv[OWN1:L2, :] = dot(pools(256, (2,)), kvo[:, 0:LANES]).astype(BF16)
    a4[0:16, :] = dot(pools(256, (16,)), kvo[:, 0:LANES]).astype(BF16)

    def xy_sends(half):
        copies = [send(a4.at[64 * half:64 * half + 64, :], kv.at[L4 + 64 * half:L4 + 64 * half + 64, :], xy_peer[1])]
        for m in range(2, 4):
            low = L5 + 64 * (m - 2) + 32 * half
            copies.append(send(a5.at[32 * half:32 * half + 32, :], kv.at[low:low + 32, :], xy_peer[m]))
        for m in range(4, 8):
            low = L6 + 32 * (m - 4) + 16 * half
            copies.append(send(a6.at[16 * half:16 * half + 16, :], kv.at[low:low + 16, :], xy_peer[m]))
        return copies

    for copy in in3:
        copy.wait_recv()
    upper = dot(pools(128, (2, 4, 8)), kv[L3:L4, :]).astype(BF16)
    a4[64:128, :] = upper[0:64]
    a5[32:64, :] = upper[64:96]
    a6[16:32, :] = upper[96:112]
    far = xy_sends(1)

    for copy in load_rest:
        copy.wait()
    in_g.wait_recv()
    ga[...] = (
        dot(gown[...], w[:, my_cols], ((1,), (1,))) + dot(gfar[...], w[:, far_cols], ((1,), (1,)))
    ).astype(BF16)
    in_ga = [send(ga.at[:, cols(j)], at_pair(gc, j), pair_peer[j]) for j in range(2, 4)]
    in_ga_core = [send(ga.at[:, cols(1)], at_pair(gc, 1), other), send(ga.at[:, cols(3)], at_pair(gm, 1), other)]
    gc[0:128, :] = ga[:, cols(0)]
    gm[0:128, :] = ga[:, cols(2)]

    lane = lax.broadcasted_iota(jnp.int32, (1, 256), 1)

    def level_bias(t, h, level):
        slope = slopes[((place + t - 2 * place * t) * 2 + core) * HEADS + h]
        return (level * LOG_TWO - slope * (level + 1.0)) * LOG2E

    def key_lanes(h, t=0):
        return slice(LANES * t + h * HEAD, LANES * t + (h + 1) * HEAD)

    def value_lanes(h, t=0):
        return slice(LANES * t + QUARTER + h * HEAD, LANES * t + QUARTER + (h + 1) * HEAD)

    def queries_of(chip):
        return slice(256 * chip, 256 * chip + 256)

    def head_of(h):
        return slice(h * HEAD, (h + 1) * HEAD)

    def across_lanes(x):
        return jnp.sum(x, axis=0, keepdims=True)

    def own_stats(t, h):
        by, to = (qc, gc) if t == 0 else (qm, gm)
        u = 2 * t + h
        tops = []
        for at in (0, 128):
            rows = slice(at, at + 128)
            bias = jnp.where((lane < 128) == (at == 0), 0.0, level_bias(t, h, 0))
            s = dot(kvo[rows, key_lanes(h, t)], by[0:256, head_of(h)], ((1,), (1,))) * (ROOT * LOG2E) + bias
            scores_o[u, rows, :] = s
            tops.append(jnp.max(in_eights(s), axis=0))
        top = jnp.max(jnp.maximum(tops[0], tops[1]), axis=0, keepdims=True)
        total = jnp.zeros((8, 256), F32)
        center = jnp.zeros((8, 256), F32)
        for at in (0, 128):
            rows = slice(at, at + 128)
            e = jnp.exp2(scores_o[u, rows, :] - top)
            scores_o[u, rows, :] = e
            toward = dot(kvo[rows, value_lanes(h, t)], to[0:256, head_of(h)], ((1,), (1,)))
            gradw_o[u, rows, :] = toward
            total = total + jnp.sum(in_eights(e), axis=0)
            center = center + jnp.sum(in_eights(e * toward), axis=0)
        return top, across_lanes(total), across_lanes(center)

    for copy in in_mate + in2:
        copy.wait_recv()
    a4[16:32, :] = dot(pools(32, (2,)), mate3[...]).astype(BF16)
    a4[32:64, :] = dot(pools(128, (4,)), kv[L2:L3, :]).astype(BF16)
    upper = dot(pools(64, (2, 4)), a4[0:64, :]).astype(BF16)
    a5[0:32, :] = upper[0:32]
    a6[0:16, :] = upper[32:48]
    far += xy_sends(0)

    for copy in in_q_core + in_ga_core:
        copy.wait_recv()
    near_stats = [own_stats(0, h) for h in range(HEADS)]

    for h in range(HEADS):
        for n, stat in enumerate(own_stats(1, h)):
            stat_out[3 * h + n:3 * h + n + 1, :] = stat
    in_stat = send(stat_out, stat_in, z_peer[1][0])

    def key_row(chip, at):
        return L1 + 128 * chip if at == S1 else L2 + at - S2

    def exponents(unit, places):
        h, chip = unit
        own = queries_of(chip)
        tops = []
        for at in places:
            row = key_row(chip, at)
            s = dot(kv[row:row + 128, key_lanes(h)], qc[own, head_of(h)], ((1,), (1,))) * (ROOT * LOG2E)
            s = s + level_bias(0, h, at // 128 + 1)
            scores[h, at:at + 128, own] = s
            tops.append(jnp.max(in_eights(s), axis=0))
        top = jnp.max(functools.reduce(jnp.maximum, tops), axis=0, keepdims=True)
        total = jnp.zeros((8, 256), F32)
        for at in places:
            e = jnp.exp2(scores[h, at:at + 128, own] - top)
            scores[h, at:at + 128, own] = e
            total = total + jnp.sum(in_eights(e), axis=0)
        return top, across_lanes(total)

    def toward_center(unit, places):
        h, chip = unit
        own = queries_of(chip)
        center = jnp.zeros((8, 256), F32)
        for at in places:
            row = key_row(chip, at)
            toward = dot(kv[row:row + 128, value_lanes(h)], gc[own, head_of(h)], ((1,), (1,)))
            gradw[h, at:at + 128, own] = toward
            center = center + jnp.sum(in_eights(scores[h, at:at + 128, own] * toward), axis=0)
        return across_lanes(center)

    units = [(h, chip) for chip in range(2) for h in range(HEADS)]
    parts = ((S2, S3), (S4, S5, S6), (S1,))
    tops, totals, sums = ({unit: {} for unit in units} for _ in range(3))

    def add_exponents(unit, n):
        tops[unit][n], totals[unit][n] = exponents(unit, parts[n])

    def add_center(unit, n):
        sums[unit][n] = toward_center(unit, parts[n])

    for unit in units[0:2]:
        add_exponents(unit, 0)
        add_center(unit, 0)
    for copy in in_q:
        copy.wait_recv()
    for unit in units[2:4]:
        add_exponents(unit, 0)
        add_exponents(unit, 2)
    in_stat.wait_recv()
    for copy in in_ga:
        copy.wait_recv()
    for unit in units[2:4]:
        add_center(unit, 0)
        add_center(unit, 2)
    for copy in far:
        copy.wait_recv()
    for unit in units[2:4] + units[0:2]:
        add_exponents(unit, 1)
        add_center(unit, 1)
    for copy in in1:
        copy.wait_recv()
    for unit in units[0:2]:
        add_exponents(unit, 2)
        add_center(unit, 2)

    scales, centers = {}, {}
    for unit in units:
        h, chip = unit
        if chip == 0:
            stat = near_stats[h]
        else:
            stat = tuple(stat_in[3 * h + n:3 * h + n + 1, :] for n in range(3))
        every = [tops[unit][n] for n in range(3)] + [stat[0]]
        masses = [totals[unit][n] for n in range(3)] + [stat[1]]
        weighted = [sums[unit][n] for n in range(3)] + [stat[2]]
        best = functools.reduce(jnp.maximum, every)
        factors = [jnp.exp2(top - best) for top in every]
        inverse = 1.0 / sum(f * mass for f, mass in zip(factors, masses))
        centers[unit] = sum(f * part for f, part in zip(factors, weighted)) * inverse
        scales[unit] = [f * inverse for f in factors]
        if chip == 1:
            final_out[2 * h:2 * h + 1, :] = scales[unit][3]
            final_out[2 * h + 1:2 * h + 2, :] = centers[unit]
    in_final = send(final_out, final_in, z_peer[1][0])

    def normalise(h, chip, n):
        own = queries_of(chip)
        for at in parts[n]:
            weight = scores[h, at:at + 128, own] * scales[h, chip][n]
            prob[h, at:at + 128, own] = weight.astype(BF16)
            dsc[h, at:at + 128, own] = (weight * (gradw[h, at:at + 128, own] - centers[h, chip])).astype(BF16)

    def gradients(h, low, high, own=slice(0, 512)):
        d_key = dot(dsc[h, low:high, own], qc[own, head_of(h)]) * ROOT
        d_value = dot(prob[h, low:high, own], gc[own, head_of(h)])
        return d_key, d_value

    def piece(low, rows):
        return out.at[low:low + rows, :]

    def to_queries(h, chip, lanes, weights):
        own, level1 = queries_of(chip), key_row(chip, S1)
        total = dot(kv[L2:ROWS, lanes], weights[h, S2:KEYS, own], ((0,), (0,)))
        return (total + dot(kv[level1:level1 + 128, lanes], weights[h, S1:S2, own], ((0,), (0,)))).T

    for h in range(HEADS):
        for n in range(3):
            normalise(h, 1, n)
        far_attn[:, head_of(h)] = to_queries(h, 1, value_lanes(h), prob).astype(BF16)
    in_rest_attn = [send(at_pair(far_attn, i), rest_attn.at[i], pair_peer[2 + i]) for i in range(2)]
    for h in range(HEADS):
        far_q[:, head_of(h)] = (to_queries(h, 1, key_lanes(h), dsc) * ROOT).astype(BF16)
    in_rest_q = [send(at_pair(far_q, i), rest_q.at[i], pair_peer[2 + i]) for i in range(2)]

    for h in range(HEADS):
        normalise(h, 0, 1)
        d_key, d_value = gradients(h, S4, KEYS)
        out[S4:KEYS, key_lanes(h)] = d_key.astype(BF16)
        out[S4:KEYS, value_lanes(h)] = d_value.astype(BF16)

    def xy_back(half):
        copies = [send(piece(S4 + 64 * half, 64), back.at[half, 0:64, :], xy_peer[1])]
        for m in range(2, 4):
            at = 64 + 32 * (m - 2)
            copies.append(send(piece(S5 + 64 * (m - 2) + 32 * half, 32), back.at[half, at:at + 32, :], xy_peer[m]))
        for m in range(4, 8):
            at = 128 + 16 * (m - 4)
            copies.append(send(piece(S6 + 32 * (m - 4) + 16 * half, 16), back.at[half, at:at + 16, :], xy_peer[m]))
        return copies

    back_near = xy_back(0)
    back_far = xy_back(1)

    for h in range(HEADS):
        normalise(h, 0, 0)
        normalise(h, 0, 2)
    for h in range(HEADS):
        d_key, d_value = gradients(h, S2, S4)
        out123[128:384, key_lanes(h)] = d_key
        out123[128:384, value_lanes(h)] = d_value
        d_key, d_value = gradients(h, S1, S2, queries_of(0))
        out123[0:128, key_lanes(h)] = d_key
        out123[0:128, value_lanes(h)] = d_value

    double = spread(256, ((2, 128, 1),))
    in_near = []
    for t in range(2):
        if t == 1:
            in_final.wait_recv()
        by, to = (qc, gc) if t == 0 else (qm, gm)
        for h in range(HEADS):
            u = 2 * t + h
            if t == 0:
                scale, center = scales[h, 0][3], centers[h, 0]
            else:
                scale, center = final_in[2 * h:2 * h + 1, :], final_in[2 * h + 1:2 * h + 2, :]
            weight = scores_o[u] * scale
            prob_o[u] = weight.astype(BF16)
            dsc_o[u] = (weight * (gradw_o[u] - center)).astype(BF16)
            for weights, source, beyond, lanes, factor in (
                (dsc_o, by, dsc, key_lanes(h, t), ROOT), (prob_o, to, prob, value_lanes(h, t), 1.0)
            ):
                total = dot(weights[u], source[0:256, head_of(h)])
                if t == 0:
                    level1 = dot(double, beyond[h, S1:S2, 256:512]).astype(BF16)
                    total = total + dot(level1, source[256:512, head_of(h)])
                acc[:, lanes] = total * factor
            attn_part = dot(kvo[:, value_lanes(h, t)], prob_o[u], ((0,), (0,))).T
            q_part = dot(kvo[:, key_lanes(h, t)], dsc_o[u], ((0,), (0,))).T
            if t == 0:
                attn_part = attn_part + to_queries(h, 0, value_lanes(h), prob)
                q_part = q_part + to_queries(h, 0, key_lanes(h), dsc)
            near_attn[t, :, head_of(h)] = attn_part.astype(BF16)
            near_q[t, :, head_of(h)] = (q_part * ROOT).astype(BF16)
        if t == 0:
            in_near += [send(near_attn.at[0, 128:256, :], whole.at[:, cols(0)], other)]
            in_near += [send(near_q.at[0, 128:256, :], grad_q.at[:, cols(0)], other)]
        else:
            in_near += [send(near_attn.at[1, 128:256, :], rest_attn.at[2], other)]
            in_near += [send(near_q.at[1, 128:256, :], rest_q.at[2], other)]

    for copy in back_near:
        copy.wait_recv()
    g4 = dot(spread(64, ((1, 64, 1), (2, 32, 2), (4, 16, 4))), back[0]).astype(BF16)
    out[0:128, :] = (out123[0:128, :] + dot(spread(128, ((8, 16, 1),)), g4[16:32])).astype(BF16)
    out[128:256, :] = (out123[128:256, :] + dot(spread(128, ((4, 32, 1),)), g4[32:64])).astype(BF16)
    home = [
        send(piece(S2 + (2 * i + sub) * 32, 32), zin.at[2 * (m % 2) + sub, 64:96, :], z_peer[m][sub])
        for i, m in enumerate((2, 3))
        for sub in range(2)
    ]
    home += [send(piece(S1 + 64 * 0, 64), zin.at[2 + 0, 0:64, :], z_peer[1][0])]
    home += [send(piece(S1 + 64 * 1, 64), zin.at[2 + 1, 0:64, :], z_peer[1][1])]
    acc[:, 0:LANES] += dot(spread(256, ((16, 16, 1),)), g4[0:16])
    home += [send(acc.at[128:256, :], acc_core, other)]

    whole[:, cols(0)] = near_attn[0, 0:128, :]
    grad_q[:, cols(0)] = near_q[0, 0:128, :]
    for copy in in_near + in_rest_attn:
        copy.wait_recv()
    whole[:, cols(2)] = (near_attn[1, 0:128, :].astype(F32) + rest_attn[0].astype(F32)).astype(BF16)
    whole[:, cols(3)] = (rest_attn[2].astype(F32) + rest_attn[1].astype(F32)).astype(BF16)
    send_part[...] = dot(whole[...], w[:, far_cols]).astype(BF16)
    part = send(send_part, recv_part, across)
    for copy in back_far:
        copy.wait_recv()
    mix = spread(128, ((2, 64, 1), (4, 32, 2), (8, 16, 4)))
    out[S3:S4, :] = (out123[256:384, :] + dot(mix, back[1])).astype(BF16)
    home += [
        send(
            piece(S3 + (2 * i + sub) * 16, 16),
            zin.at[2 * (m % 2) + sub, 96 + 16 * (i // 2):112 + 16 * (i // 2), :],
            z_peer[m][sub],
        )
        for i, m in enumerate((4, 5, 6, 7))
        for sub in range(2)
    ]

    for copy in in_rest_q:
        copy.wait_recv()
    grad_q[:, cols(2)] = (near_q[1, 0:128, :].astype(F32) + rest_q[0].astype(F32)).astype(BF16)
    grad_q[:, cols(3)] = (rest_q[2].astype(F32) + rest_q[1].astype(F32)).astype(BF16)
    own_part = dot(whole[...], w[:, my_cols])
    part.wait_recv()
    layer_out[...] = (own_part + recv_part[...].astype(F32)).astype(BF16)

    mix = spread(128, ((2, 64, 1), (4, 32, 1), (8, 16, 2)))
    for copy in home[:-8]:
        copy.wait_recv()
    bases = (acc[0:128, 0:LANES], acc_core[:, 0:LANES], acc[0:128, LANES:1024], acc_core[:, LANES:1024])
    for j, base in enumerate(bases):
        low = 64 if j < 2 else 0
        early[j] = base + dot(mix[:, low:96], zin[j, low:96, :])
    for copy in home[-8:]:
        copy.wait_recv()
    for j in range(4):
        total = (early[j] + dot(mix[:, 96:128], zin[j, 96:128, :])).astype(BF16)
        grad_k[:, cols(j)] = total[:, 0:QUARTER]
        grad_v[:, cols(j)] = total[:, QUARTER:LANES]
    for copy in started:
        copy.wait_send()


COPIES = 96


def store(*refs):
    sems = refs[8]
    copies = [pltpu.make_async_copy(refs[i], refs[4 + i], sems.at[i]) for i in range(4)]
    for copy in copies:
        copy.start()
    for copy in copies:
        copy.wait()


def local(queries, key_vectors, value_vectors, slopes, w_out, grad_out):
    block = jax.ShapeDtypeStruct((B, 1024), BF16)
    vmem = pl.BlockSpec(memory_space=pltpu.VMEM)
    hbm = pl.BlockSpec(memory_space=pltpu.HBM)
    arguments = (slopes, queries, key_vectors, value_vectors, grad_out, w_out)
    results = pl.pallas_call(
        kernel,
        out_shape=[pltpu.VMEM((B, 1024), BF16)] * 4,
        in_specs=[hbm] * 6,
        out_specs=[vmem] * 4,
        scratch_shapes=[
            pltpu.SMEM((8,), F32),
            pltpu.VMEM((ROWS, LANES), BF16),
            pltpu.VMEM((256, 1024), BF16),
            pltpu.VMEM((128, 1024), BF16),
            pltpu.VMEM((512, QUARTER), BF16),
            pltpu.VMEM((256, QUARTER), BF16),
            pltpu.VMEM((512, QUARTER), BF16),
            pltpu.VMEM((256, QUARTER), BF16),
            pltpu.VMEM((128, 1024), BF16),
            pltpu.VMEM((128, 1024), BF16),
            pltpu.VMEM((1024, 2048), BF16),
            pltpu.VMEM((4, 64, LANES), BF16),
            pltpu.VMEM((4, 32, LANES), BF16),
            pltpu.VMEM((4, 16, LANES), BF16),
            pltpu.VMEM((32, LANES), BF16),
            pltpu.VMEM((128, LANES), BF16),
            pltpu.VMEM((64, LANES), BF16),
            pltpu.VMEM((32, LANES), BF16),
            pltpu.VMEM((HEADS, KEYS, 512), F32),
            pltpu.VMEM((HEADS, KEYS, 512), F32),
            pltpu.VMEM((HEADS, KEYS, 512), BF16),
            pltpu.VMEM((HEADS, KEYS, 512), BF16),
            pltpu.VMEM((4, 256, 256), F32),
            pltpu.VMEM((4, 256, 256), F32),
            pltpu.VMEM((4, 256, 256), BF16),
            pltpu.VMEM((4, 256, 256), BF16),
            pltpu.VMEM((8, 256), F32),
            pltpu.VMEM((8, 256), F32),
            pltpu.VMEM((8, 256), F32),
            pltpu.VMEM((8, 256), F32),
            pltpu.VMEM((KEYS, LANES), BF16),
            pltpu.VMEM((384, LANES), F32),
            pltpu.VMEM((2, 192, LANES), BF16),
            pltpu.VMEM((4, 128, LANES), BF16),
            pltpu.VMEM((256, 1024), F32),
            pltpu.VMEM((128, 1024), F32),
            pltpu.VMEM((4, 128, LANES), F32),
            pltpu.VMEM((256, QUARTER), BF16),
            pltpu.VMEM((256, QUARTER), BF16),
            pltpu.VMEM((2, 256, QUARTER), BF16),
            pltpu.VMEM((2, 256, QUARTER), BF16),
            pltpu.VMEM((3, 128, QUARTER), BF16),
            pltpu.VMEM((3, 128, QUARTER), BF16),
            pltpu.VMEM((128, 1024), BF16),
            pltpu.VMEM((128, 1024), BF16),
            pltpu.VMEM((128, 1024), BF16),
            pltpu.VMEM((128, 1024), BF16),
            pltpu.SemaphoreType.DMA((COPIES,)),
            pltpu.SemaphoreType.DMA((COPIES,)),
            pltpu.SemaphoreType.DMA((13,)),
        ],
        compiler_params=pltpu.CompilerParams(
            collective_id=0, has_side_effects=True, vmem_limit_bytes=48 * 1024 * 1024
        ),
        cost_estimate=pl.CostEstimate(flops=2_700_000_000, bytes_accessed=8_000_000, transcendentals=1_000_000),
    )(*(pltpu.with_memory_space_constraint(x, pltpu.HBM) for x in arguments))
    return pl.pallas_call(
        store,
        out_shape=[block] * 4,
        in_specs=[vmem] * 4,
        out_specs=[hbm] * 4,
        scratch_shapes=[pltpu.SemaphoreType.DMA((4,))],
    )(*(pltpu.with_memory_space_constraint(x, pltpu.VMEM) for x in results))


def solution(mesh):
    cut = P("ctx", "head")
    return jax.shard_map(
        local,
        mesh=mesh,
        in_specs=(cut, cut, cut, P("head"), P("head", None), cut),
        out_specs=(cut, cut, cut, cut),
        check_vma=False,
    )
```
